512 devices in a mesh: seq: 16 (over z), tensor: 8 (over x, core), dp: 4 (over y).
Axes of the slice: x: 4, y: 4, z: 16, core: 2. Of those that a mesh axis runs over, the one named last changes fastest.
Arguments:
- query_rows: bfloat16 [4, 2048, 8192], P('dp', ('seq', 'tensor')), may hold values from -2 to 2
- key_rows: bfloat16 [4, 2048, 8192], P('dp', ('seq', 'tensor')), may hold values from -2 to 2
- value_rows: bfloat16 [4, 2048, 8192], P('dp', ('seq', 'tensor')), may hold values from -6 to 6
- cotangent: bfloat16 [4, 2048, 8192], P('dp', ('seq', 'tensor')), may hold values from -6 to 6
- norm_gain: float32 [8192], P('tensor'), may hold values from 0.25 to 1.75
- doc_starts: int32 [4, 8], P('dp'), may hold values from 0 to 2047, as said below
Outputs:
- query_grad: bfloat16 [4, 2048, 8192], P('dp', ('seq', 'tensor'))
- key_grad: bfloat16 [4, 2048, 8192], P('dp', ('seq', 'tensor'))
- value_grad: bfloat16 [4, 2048, 8192], P('dp', ('seq', 'tensor'))
- gain_grad: float32 [8192], P('tensor')
The draws below stay inside these ranges and needn't reach their ends.
Inputs may be any that keep to these rules, and one draw needn't show every extreme that they name: `doc_starts`: each row is strictly increasing, begins with 0 and ends with 2047.
All inputs are finite; a program needn't handle non-finite values.
Results may differ from the reference program's by a relative error of at most 0.0015.
Values may be sent and summed in bfloat16 or wider, within the bound.
A program may use at most 64 MiB of HBM per device.

```python
import math
import jax
import jax.numpy as jnp
from jax import lax

HEADS = 64
HEAD_DIM = 128
TOK_DEV = 128
HD = 8192
SEQ_LEN = 2048
BATCH = 4
NDOC = 8


def shared_part(key):
    return jax.random.normal(key, (BATCH, SEQ_LEN, HD), jnp.float32)


def draw_query_rows(key, part):
    common = shared_part(key)
    key = jax.random.fold_in(key, 11)
    noise = jax.random.normal(key, (BATCH, SEQ_LEN, HD), jnp.float32)
    return jnp.clip(0.25 * common + 0.15 * noise, -2.0, 2.0).astype(jnp.bfloat16)


def draw_key_rows(key, part):
    common = shared_part(key)
    key = jax.random.fold_in(key, 12)
    noise = jax.random.normal(key, (BATCH, SEQ_LEN, HD), jnp.float32)
    return jnp.clip(0.25 * common + 0.15 * noise, -2.0, 2.0).astype(jnp.bfloat16)


def draw_doc_starts(key, part):
    key = jax.random.fold_in(key, 13)
    row_keys = jax.random.split(key, BATCH)

    def one_row(row_key):
        picks = jax.random.permutation(row_key, SEQ_LEN - 2)[:NDOC - 2] + 1
        first = jnp.zeros((1,), jnp.int32)
        final = jnp.full((1,), SEQ_LEN - 1, jnp.int32)
        return jnp.concatenate([first, jnp.sort(picks).astype(jnp.int32), final])
    return jax.vmap(one_row)(row_keys).astype(jnp.int32)


def steps_of(key, shape, cuts, least, high):
    gain, own = 1.0, jax.random.fold_in(key, 6)
    for position, blocks in cuts:
        draws = jnp.exp(jax.random.uniform(jax.random.fold_in(own, position), (blocks,), jnp.float32, least / len(cuts), high / len(cuts)))
        gain = gain * jnp.repeat(draws, shape[position] // blocks).reshape([-1 if axis == position else 1 for axis in range(len(shape))])
    return gain


def centred(own_key, dims, scale, reach, cuts=(), kind=jnp.bfloat16):
    drawn = scale * jax.random.normal(own_key, dims, jnp.float32)
    if cuts:
        drawn = drawn * steps_of(own_key, dims, cuts, -0.22, 0.18)
    return jnp.clip(drawn, -reach, reach).astype(kind)


def setup_inputs(seed: int = 0) -> dict:
    keys = jax.random.split(jax.random.key(seed), 7)
    return {
        "query_rows": draw_query_rows(jax.random.fold_in(keys[6], 71), 0),
        "key_rows": draw_key_rows(jax.random.fold_in(keys[6], 71), 0),
        "value_rows": centred(keys[2], (BATCH, SEQ_LEN, HD), 1.0, 6.0, ((0, 4), (1, 128))),
        "cotangent": centred(keys[3], (BATCH, SEQ_LEN, HD), 1.0, 6.0, ((0, 4), (1, 128))),
        "norm_gain": jnp.clip(1.0 + 0.15 * jax.random.normal(keys[4], (HD,), jnp.float32), 0.25, 1.75),
        "doc_starts": draw_doc_starts(jax.random.fold_in(keys[6], 71), 0),
    }


EPSILON = 1e-05
HIGHEST = lax.Precision.HIGHEST

def segment_of(positions, starts_row):
    return lax.optimization_barrier(jnp.sum((starts_row[None, :] <= positions[:, None]).astype(jnp.int32), axis=1)) - 1

def head_forward(query_f, key_f, value_f, gain_row, segment):
    blocks = SEQ_LEN // TOK_DEV
    query_blk = query_f.reshape(blocks, TOK_DEV, HEAD_DIM)
    key_blk = key_f.reshape(blocks, TOK_DEV, HEAD_DIM)
    value_blk = value_f.reshape(blocks, TOK_DEV, HEAD_DIM)
    seg_blk = segment.reshape(blocks, TOK_DEV)
    prev_seg = jnp.concatenate([jnp.full((1,), -1, jnp.int32), seg_blk[:-1, -1].astype(jnp.int32)])
    rows_idx = jnp.arange(TOK_DEV, dtype=jnp.int32)
    causal = rows_idx[:, None] >= rows_idx[None, :]

    def step(state, inputs):
        query_b, key_b, value_b, seg_b, prev_b = inputs
        doc_mask = (causal & (seg_b[:, None] == seg_b[None, :])).astype(jnp.float32)
        scores = jnp.dot(query_b, key_b.T, precision=HIGHEST) * doc_mask
        uses_state = (seg_b == prev_b).astype(jnp.float32)
        result = jnp.dot(scores, value_b, precision=HIGHEST)
        result = result + uses_state[:, None] * jnp.dot(query_b, state, precision=HIGHEST)
        keep_key = (seg_b == seg_b[-1]).astype(jnp.float32)
        carry_flag = (prev_b == seg_b[-1]).astype(jnp.float32)
        new_state = jnp.dot((key_b * keep_key[:, None]).T, value_b, precision=HIGHEST) + carry_flag * state
        return (new_state, result)
    start_state = jnp.zeros((HEAD_DIM, HEAD_DIM), jnp.float32)
    final_state, results = lax.scan(step, start_state, (query_blk, key_blk, value_blk, seg_blk, prev_seg))
    attended = results.reshape(SEQ_LEN, HEAD_DIM)
    centre = lax.optimization_barrier(jnp.mean(attended, axis=-1, keepdims=True))
    centered = attended - centre
    spread = lax.optimization_barrier(jnp.mean(centered * centered, axis=-1, keepdims=True))
    normed = centered * lax.rsqrt(spread + EPSILON)
    return normed * gain_row[None, :]

def reference(query_rows, key_rows, value_rows, cotangent, norm_gain, doc_starts):

    def split_heads(array):
        return array.reshape(BATCH, SEQ_LEN, HEADS, HEAD_DIM).transpose(0, 2, 1, 3).reshape(BATCH * HEADS, SEQ_LEN, HEAD_DIM)

    def merge_heads(array):
        return array.reshape(BATCH, HEADS, SEQ_LEN, HEAD_DIM).transpose(0, 2, 1, 3).reshape(BATCH, SEQ_LEN, HD).astype(jnp.bfloat16)
    starts_items = jnp.repeat(doc_starts, HEADS, axis=0)
    gain_items = jnp.tile(norm_gain.reshape(HEADS, HEAD_DIM), (BATCH, 1))

    def one_item(item):
        query_x, key_x, value_x, cot_x, gain_x, starts_x = item
        segment = segment_of(jnp.arange(SEQ_LEN, dtype=jnp.int32), starts_x)

        def forward(query_f, key_f, value_f, gain_row):
            return head_forward(query_f, key_f, value_f, gain_row, segment)
        output, pullback = jax.vjp(forward, query_x.astype(jnp.float32), key_x.astype(jnp.float32), value_x.astype(jnp.float32), gain_x)
        return pullback(cot_x.astype(jnp.float32))
    items = (split_heads(query_rows), split_heads(key_rows), split_heads(value_rows), split_heads(cotangent), gain_items, starts_items)
    grad_q, grad_k, grad_v, grad_g = lax.map(one_item, items)
    gain_grad = lax.optimization_barrier(jnp.sum(grad_g.reshape(BATCH, HD), axis=0)) / math.sqrt(BATCH * SEQ_LEN)
    return (merge_heads(grad_q), merge_heads(grad_k), merge_heads(grad_v), gain_grad)
```

```python
import functools
import math

import jax
import jax.numpy as jnp
from jax import lax
from jax.experimental import pallas as pl
from jax.experimental.pallas import tpu as pltpu
from jax.sharding import PartitionSpec as P

MESH = pl.DeviceIdType.MESH
F32 = jnp.float32
BF16 = jnp.bfloat16
EPSILON = 1e-05
DIM = 128
HEADS = 4
TOK = 256
COLS = HEADS * DIM
ROWS = 16
GROUP = 16
SEQ = 16
PAIRS = 8
SUB = 4
PIECE = DIM // SUB
NC = HEADS * SUB


def split(x):
    hi = x.astype(BF16)
    return hi, (x - hi.astype(F32)).astype(BF16)


def mm(a, b, ca=1, cb=0):
    return lax.dot_general(a, b, (((ca,), (cb,)), ((), ())), preferred_element_type=F32)


def kernel(
    k_ref, v_ref, q_ref, c_ref, gain_ref, starts_ref,
    out_ref, gout_ref,
    buf, mask, use, keep, own, frecv, fsend, brecv, bsend, scores, dh, dl, dkl, dvl, obuf,
    gsrc, gy, gz,
    in_send, in_recv, f_send, f_recv, b_send, b_recv, o_send, o_recv,
    gy_send, gy_recv, gz_send, gz_recv,
):
    z, t, y = lax.axis_index("seq"), lax.axis_index("tensor"), lax.axis_index("dp")
    p, j = z // 2, lax.rem(z, 2)
    base = p * 2
    me = j * 8 + t
    after, before = lax.rem(z + 2, SEQ), lax.rem(z + SEQ - 2, SEQ)

    def peer(s):
        g = lax.rem(me + s, GROUP)
        return g, g // 8, lax.rem(g, 8)

    barrier = pltpu.get_barrier_semaphore()

    def greet(zz, tt, yy):
        pl.semaphore_signal(barrier, inc=1, device_id=(zz, tt, yy), device_id_type=MESH)

    def greet_group(s, _):
        _, jj, tt = peer(s)
        greet(base + jj, tt, y)
        return 0

    lax.fori_loop(1, GROUP, greet_group, 0)

    def greet_seq(s, _):
        zz = lax.rem(base + s, SEQ)
        greet(zz, t, y)
        return 0

    lax.fori_loop(2, SEQ, greet_seq, 0)
    for s in range(1, 4):
        greet(z, t, lax.rem(y + s, 4))
    pl.semaphore_wait(barrier, 15 + 14 + 3)

    def send_in(refs):
        def body(s, _):
            _, jj, tt = peer(s)
            col = pl.multiple_of(tt * 1024 + jj * COLS, DIM)
            for a, ref in refs:
                pltpu.make_async_remote_copy(
                    src_ref=ref.at[0, :, pl.ds(col, COLS)],
                    dst_ref=buf.at[a, pl.ds(pl.multiple_of(me * ROWS, ROWS), ROWS), :],
                    send_sem=in_send.at[a],
                    recv_sem=in_recv.at[a],
                    device_id=(base + jj, tt, y),
                    device_id_type=MESH,
                ).start()
            return 0

        lax.fori_loop(1, GROUP, body, 0)
        for a, ref in refs:
            pltpu.make_async_copy(
                ref.at[0, :, pl.ds(pl.multiple_of(t * 1024 + j * COLS, DIM), COLS)],
                buf.at[a, pl.ds(pl.multiple_of(me * ROWS, ROWS), ROWS), :],
                in_recv.at[a],
            ).start()

    def wait_in(a):
        pltpu.make_async_copy(buf.at[a], buf.at[a], in_recv.at[a]).wait()

    send_in(((0, k_ref), (1, v_ref)))
    send_in(((2, q_ref), (3, c_ref)))

    def count(tok):
        total = jnp.zeros_like(tok)
        for i in range(8):
            total = total + (starts_ref[0, i] <= tok).astype(jnp.int32)
        return total

    first = base * 128
    prev = count(first - 1)
    last = count(first + TOK - 1)
    carry = (prev == last).astype(F32)
    row = lax.broadcasted_iota(jnp.int32, (TOK, DIM), 0) + first
    seg = count(row)
    use[...] = (seg == prev).astype(F32)
    keep[...] = (seg == last).astype(F32)
    seg_row = count(lax.broadcasted_iota(jnp.int32, (8, TOK), 1) + first)[:1]
    seg_col = jnp.concatenate([seg, seg], axis=1)
    rows = lax.broadcasted_iota(jnp.int32, (TOK, TOK), 0)
    cols = lax.broadcasted_iota(jnp.int32, (TOK, TOK), 1)
    mask[...] = ((rows >= cols) & (seg_col == seg_row)).astype(F32)
    gsrc[...] = jnp.zeros_like(gsrc)

    @pl.when(p == 0)
    def _():
        frecv[...] = jnp.zeros_like(frecv)

    @pl.when(p == PAIRS - 1)
    def _():
        brecv[...] = jnp.zeros_like(brecv)

    def take(a, h):
        return buf[a, :, pl.ds(pl.multiple_of(h * DIM, DIM), DIM)]

    wait_in(0)
    wait_in(1)

    def local_state(h, _):
        kept = take(0, h) * keep[...].astype(BF16)
        own[h] = mm(kept, take(1, h), 0, 0)
        return 0

    lax.fori_loop(0, HEADS, local_state, 0)

    def piece(ref, c):
        return ref.at[c // SUB, pl.ds(pl.multiple_of(lax.rem(c, SUB) * PIECE, PIECE), PIECE), :]

    def fcopy(c):
        return pltpu.make_async_remote_copy(
            src_ref=piece(fsend, c), dst_ref=piece(frecv, c),
            send_sem=f_send.at[c], recv_sem=f_recv.at[c],
            device_id=(after, t, y), device_id_type=MESH,
        )

    def bcopy(c):
        return pltpu.make_async_remote_copy(
            src_ref=piece(bsend, c), dst_ref=piece(brecv, c),
            send_sem=b_send.at[c], recv_sem=b_recv.at[c],
            device_id=(before, t, y), device_id_type=MESH,
        )

    def forward(c, _):
        @pl.when(p > 0)
        def _():
            fcopy(c).wait_recv()

        @pl.when(p < PAIRS - 1)
        def _():
            piece(fsend, c)[...] = piece(own, c)[...] + carry * piece(frecv, c)[...]
            fcopy(c).start()

        return 0

    def local_scores(h, _):
        scores[h] = mm(take(2, h), take(0, h), 1, 1) * mask[...]
        return 0

    def first_half(s, _):
        @pl.when((s == 0) == (p < PAIRS // 2))
        def _():
            lax.fori_loop(0, NC, forward, 0)

        @pl.when((s == 0) != (p < PAIRS // 2))
        def _():
            wait_in(2)
            lax.fori_loop(0, HEADS, local_scores, 0)

        return 0

    lax.fori_loop(0, 2, first_half, 0)
    wait_in(3)

    def attend(h, _):
        query, value = take(2, h), take(1, h)
        sh, sl = split(scores[h])
        th, tl = split(frecv[h])
        att = mm(sh, value) + mm(sl, value) + use[...] * (mm(query, th) + mm(query, tl))
        centered = att - jnp.mean(att, axis=-1, keepdims=True)
        inv = lax.rsqrt(jnp.mean(centered * centered, axis=-1, keepdims=True) + EPSILON)
        normed = centered * inv
        up = take(3, h).astype(F32)
        at = j * HEADS + h
        gsrc[pl.ds(at, 1), :] = jnp.sum(up * normed, axis=0, keepdims=True)
        dn = up * gain_ref[pl.ds(at, 1), :]
        d_att = inv * (
            dn
            - jnp.mean(dn, axis=-1, keepdims=True)
            - normed * jnp.mean(dn * normed, axis=-1, keepdims=True)
        )
        hi, lo = split(d_att)
        dh[h] = hi
        dl[h] = lo
        used = use[...].astype(BF16)
        bsend[h] = mm(query, hi * used, 0, 0) + mm(query, lo * used, 0, 0)

        @pl.when(p == PAIRS - 1)
        def _():
            for s in range(SUB):
                bcopy(h * SUB + s).start()

        return 0

    lax.fori_loop(0, HEADS, attend, 0)

    gy[y] = gsrc[...]

    def gy_copy(yy):
        return pltpu.make_async_remote_copy(
            src_ref=gy.at[y], dst_ref=gy.at[y], send_sem=gy_send.at[yy], recv_sem=gy_recv.at[y],
            device_id=(z, t, yy), device_id_type=MESH,
        )

    for s in range(1, 4):
        gy_copy(lax.rem(y + s, 4)).start()

    def backward(c, _):
        @pl.when(p < PAIRS - 1)
        def _():
            bcopy(c).wait_recv()

            @pl.when(p > 0)
            def _():
                piece(bsend, c)[...] += carry * piece(brecv, c)[...]
                bcopy(c).start()

        return 0

    def send_out(i):
        def body(s, _):
            g, jj, tt = peer(s)
            pltpu.make_async_remote_copy(
                src_ref=obuf.at[i, pl.ds(pl.multiple_of(g * ROWS, ROWS), ROWS), :],
                dst_ref=out_ref.at[i, :, pl.ds(pl.multiple_of(t * 1024 + j * COLS, DIM), COLS)],
                send_sem=o_send.at[i],
                recv_sem=o_recv.at[i],
                device_id=(base + jj, tt, y),
                device_id_type=MESH,
            ).start()
            return 0

        lax.fori_loop(1, GROUP, body, 0)
        pltpu.make_async_copy(
            obuf.at[i, pl.ds(pl.multiple_of(me * ROWS, ROWS), ROWS), :],
            out_ref.at[i, :, pl.ds(pl.multiple_of(t * 1024 + j * COLS, DIM), COLS)],
            o_recv.at[i],
        ).start()

    def put(i, h, value):
        obuf[i, :, pl.ds(pl.multiple_of(h * DIM, DIM), DIM)] = value.astype(BF16)

    def local_grads(h, _):
        key, value, query = take(0, h), take(1, h), take(2, h)
        hi, lo = dh[h], dl[h]
        d_sc = (mm(hi, value, 1, 1) + mm(lo, value, 1, 1)) * mask[...]
        eh, el = split(d_sc)
        th, tl = split(frecv[h])
        sh, sl = split(scores[h])
        d_query = mm(eh, key) + mm(el, key)
        d_query = d_query + use[...] * (mm(hi, th, 1, 1) + mm(hi, tl, 1, 1) + mm(lo, th, 1, 1))
        put(0, h, d_query)
        dkl[h] = mm(eh, query, 0, 0) + mm(el, query, 0, 0)
        dvl[h] = mm(sh, hi, 0, 0) + mm(sl, hi, 0, 0) + mm(sh, lo, 0, 0)
        return 0

    def second_half(s, _):
        @pl.when((s == 0) == (p >= PAIRS // 2))
        def _():
            lax.fori_loop(0, NC, backward, 0)

        @pl.when((s == 0) != (p >= PAIRS // 2))
        def _():
            lax.fori_loop(0, HEADS, local_grads, 0)
            send_out(0)

        return 0

    lax.fori_loop(0, 2, second_half, 0)

    for s in range(1, 4):
        yy = lax.rem(y + s, 4)
        pltpu.make_async_copy(gy.at[yy], gy.at[yy], gy_recv.at[yy]).wait()
    gz[z] = (gy[0] + gy[1]) + (gy[2] + gy[3])

    def gz_start(s, _):
        pltpu.make_async_remote_copy(
            src_ref=gz.at[z], dst_ref=gz.at[z], send_sem=gz_send, recv_sem=gz_recv,
            device_id=(lax.rem(z + s, SEQ), t, y), device_id_type=MESH,
        ).start()
        return 0

    def last_grads(h, _):
        key, value = take(0, h), take(1, h)
        gh, gl = split(brecv[h])
        put(1, h, dkl[h] + keep[...] * (mm(value, gh, 1, 1) + mm(value, gl, 1, 1)))
        put(2, h, dvl[h] + keep[...] * (mm(key, gh) + mm(key, gl)))
        return 0

    lax.fori_loop(0, HEADS, last_grads, 0)
    send_out(1)
    send_out(2)
    lax.fori_loop(1, SEQ, gz_start, 0)

    part = gz.at[pl.ds(0, SEQ - 1)]
    pltpu.make_async_copy(part, part, gz_recv).wait()
    total = gz[0]
    for s in range(1, SEQ):
        total = total + gz[s]
    gout_ref[...] = total / math.sqrt(4 * SEQ * 128)

    for i in range(3):
        pltpu.make_async_copy(out_ref.at[i], out_ref.at[i], o_recv.at[i]).wait()
    for a in range(4):
        part = buf.at[a, pl.ds(0, TOK - ROWS), :]
        pltpu.make_async_copy(part, part, in_send.at[a]).wait()
    for i in range(3):
        part = obuf.at[i, pl.ds(0, TOK - ROWS), :]
        pltpu.make_async_copy(part, part, o_send.at[i]).wait()
    part = gz.at[pl.ds(0, SEQ - 1)]
    pltpu.make_async_copy(part, part, gz_send).wait()
    for s in range(1, 4):
        gy_copy(lax.rem(y + s, 4)).wait_send()

    def drain(c, _):
        @pl.when(p < PAIRS - 1)
        def _():
            fcopy(c).wait_send()

        @pl.when(p > 0)
        def _():
            bcopy(c).wait_send()

        return 0

    lax.fori_loop(0, NC, drain, 0)


def place(grads_ref, gain_ref, q_ref, k_ref, v_ref, g_ref, sems):
    copies = [
        pltpu.make_async_copy(grads_ref.at[i], ref.at[0], sems.at[i])
        for i, ref in enumerate((q_ref, k_ref, v_ref))
    ]
    for copy in copies:
        copy.start()
    g_ref[...] = gain_ref[...]
    for copy in copies:
        copy.wait()


def local(query_rows, key_rows, value_rows, cotangent, norm_gain, doc_starts):
    anywhere = pl.BlockSpec(memory_space=pl.ANY)
    hbm = pl.BlockSpec(memory_space=pltpu.HBM)
    vmem = pl.BlockSpec(memory_space=pltpu.VMEM)
    smem = pl.BlockSpec(memory_space=pltpu.SMEM)
    dma = pltpu.SemaphoreType.DMA
    state = pltpu.VMEM((HEADS, DIM, DIM), F32)
    grads, gain_sum = pl.pallas_call(
        kernel,
        out_shape=(
            jax.ShapeDtypeStruct((3, ROWS, 8192), BF16),
            jax.ShapeDtypeStruct((8, DIM), F32),
        ),
        in_specs=[hbm] * 4 + [vmem, smem],
        out_specs=(anywhere, vmem),
        scratch_shapes=[
            pltpu.VMEM((4, TOK, COLS), BF16),
            pltpu.VMEM((TOK, TOK), F32),
            pltpu.VMEM((TOK, DIM), F32),
            pltpu.VMEM((TOK, DIM), F32),
            state, state, state, state, state,
            pltpu.VMEM((HEADS, TOK, TOK), F32),
            pltpu.VMEM((HEADS, TOK, DIM), BF16),
            pltpu.VMEM((HEADS, TOK, DIM), BF16),
            pltpu.VMEM((HEADS, TOK, DIM), F32),
            pltpu.VMEM((HEADS, TOK, DIM), F32),
            pltpu.VMEM((3, TOK, COLS), BF16),
            pltpu.VMEM((8, DIM), F32),
            pltpu.VMEM((4, 8, DIM), F32),
            pltpu.VMEM((SEQ, 8, DIM), F32),
            dma((4,)), dma((4,)), dma((NC,)), dma((NC,)), dma((NC,)), dma((NC,)), dma((3,)), dma((3,)),
            dma((4,)), dma((4,)), dma, dma,
        ],
        compiler_params=pltpu.CompilerParams(
            collective_id=1, has_side_effects=True, vmem_limit_bytes=60 * 1024 * 1024
        ),
        name="layer",
    )(key_rows, value_rows, query_rows, cotangent, norm_gain.reshape(8, DIM), doc_starts)
    rows = jax.ShapeDtypeStruct((1, ROWS, 8192), BF16)
    grad_q, grad_k, grad_v, gain = pl.pallas_call(
        place,
        out_shape=(rows, rows, rows, jax.ShapeDtypeStruct((8, DIM), F32)),
        in_specs=[vmem, vmem],
        out_specs=(anywhere, anywhere, anywhere, vmem),
        scratch_shapes=[dma((3,))],
        name="place",
    )(grads, gain_sum)
    return grad_q, grad_k, grad_v, gain.reshape(8 * DIM)


def solution(mesh):
    rows = P("dp", ("seq", "tensor"), None)
    return jax.shard_map(
        local,
        mesh=mesh,
        in_specs=(rows, rows, rows, rows, P("tensor"), P("dp", None)),
        out_specs=(rows, rows, rows, P("tensor")),
        check_vma=False,
    )
```

```python
import functools
import math

import jax
import jax.numpy as jnp
from jax import lax
from jax.experimental import pallas as pl
from jax.experimental.pallas import tpu as pltpu
from jax.sharding import PartitionSpec as P

MESH = pl.DeviceIdType.MESH
F32 = jnp.float32
BF16 = jnp.bfloat16
EPSILON = 1e-05
DIM = 128
HEADS = 2
GZ = 4
POS = 4
TOK = 512
HALF = 256
COLS = HEADS * DIM
ROWS = 16
GROUP = 32
SEQ = 16
SUB = 4
PIECE = DIM // SUB
NC = HEADS * SUB


def split(x):
    hi = x.astype(BF16)
    return hi, (x - hi.astype(F32)).astype(BF16)


def mm(a, b, ca=1, cb=0):
    return lax.dot_general(a, b, (((ca,), (cb,)), ((), ())), preferred_element_type=F32)


def kernel(
    k_ref, v_ref, q_ref, c_ref, gain_ref, starts_ref,
    out_ref, gout_ref,
    buf, mask, use, keep, own, fsend, rp, rm, sg, bsend, bm, bp, scores, dh, dl, dkl, dvl, obuf,
    gsrc, gy, gg, gz,
    in_send, in_recv, plus_send, rp_recv, minus_send, rm_recv, bminus_send, bm_recv, bplus_send, bp_recv,
    o_send, o_recv, gy_send, gy_recv, gg_send, gg_recv, gz_send, gz_recv,
):
    z, t, y = lax.axis_index("seq"), lax.axis_index("tensor"), lax.axis_index("dp")
    p, j = z // GZ, lax.rem(z, GZ)
    base = p * GZ
    me = j * 8 + t
    after, before = lax.rem(z + GZ, SEQ), lax.rem(z + SEQ - GZ, SEQ)

    def peer(s):
        g = lax.rem(me + s, GROUP)
        return g, g // 8, lax.rem(g, 8)

    barrier = pltpu.get_barrier_semaphore()

    def greet(zz, tt, yy):
        pl.semaphore_signal(barrier, inc=1, device_id=(zz, tt, yy), device_id_type=MESH)

    greet(after, t, y)
    greet(before, t, y)
    for s in range(1, 4):
        greet(z, t, lax.rem(y + s, 4))

    def greet_group(s, _):
        _, jj, tt = peer(s)
        greet(base + jj, tt, y)
        return 0

    lax.fori_loop(1, GROUP, greet_group, 0)

    def count(tok):
        total = jnp.zeros_like(tok)
        for i in range(8):
            total = total + (starts_ref[0, i] <= tok).astype(jnp.int32)
        return total

    first = base * 128
    prev = count(first - 1)
    last = count(first + TOK - 1)
    carry = (prev == last).astype(F32)
    far_in = (count(TOK - 1) == prev).astype(F32)
    far_out = (last == count(3 * TOK - 1)).astype(F32)
    row = lax.broadcasted_iota(jnp.int32, (TOK, DIM), 0) + first
    seg = count(row)
    use[...] = (seg == prev).astype(F32)
    keep[...] = (seg == last).astype(F32)
    seg_row = count(lax.broadcasted_iota(jnp.int32, (8, TOK), 1) + first)[:1]
    seg_col = jnp.concatenate([seg] * 4, axis=1)
    rows = lax.broadcasted_iota(jnp.int32, (TOK, TOK), 0)
    cols = lax.broadcasted_iota(jnp.int32, (TOK, TOK), 1)
    mask[...] = ((rows >= cols) & (seg_col == seg_row)).astype(F32)
    gsrc[...] = jnp.zeros_like(gsrc)

    @pl.when(p == 0)
    def _():
        rp[...] = jnp.zeros_like(rp)

    @pl.when(p <= 1)
    def _():
        rm[...] = jnp.zeros_like(rm)

    @pl.when(p == 3)
    def _():
        bm[...] = jnp.zeros_like(bm)

    @pl.when(p >= 2)
    def _():
        bp[...] = jnp.zeros_like(bp)

    pl.semaphore_wait(barrier, 31 + 2 + 3)

    mine = pl.ds(pl.multiple_of(me * ROWS, ROWS), ROWS)
    my_cols = pl.ds(pl.multiple_of(t * 1024 + j * COLS, COLS), COLS)

    def send_in(refs):
        def body(s, _):
            _, jj, tt = peer(s)
            col = pl.multiple_of(tt * 1024 + jj * COLS, COLS)
            for a, ref in refs:
                pltpu.make_async_remote_copy(
                    src_ref=ref.at[0, :, pl.ds(col, COLS)],
                    dst_ref=buf.at[a, mine, :],
                    send_sem=in_send.at[a],
                    recv_sem=in_recv.at[a],
                    device_id=(base + jj, tt, y),
                    device_id_type=MESH,
                ).start()
            return 0

        lax.fori_loop(1, GROUP, body, 0)
        for a, ref in refs:
            pltpu.make_async_copy(ref.at[0, :, my_cols], buf.at[a, mine, :], in_recv.at[a]).start()

    def wait_in(a):
        pltpu.make_async_copy(buf.at[a], buf.at[a], in_recv.at[a]).wait()

    send_in(((0, k_ref), (1, v_ref)))
    send_in(((2, q_ref), (3, c_ref)))

    def take(a, h, start=0, size=TOK):
        return buf[a, pl.ds(start, size), pl.ds(pl.multiple_of(h * DIM, DIM), DIM)]

    wait_in(0)
    wait_in(1)

    def local_state(h, _):
        kept = take(0, h) * keep[...].astype(BF16)
        own[h] = mm(kept, take(1, h), 0, 0)
        return 0

    lax.fori_loop(0, HEADS, local_state, 0)

    def piece(ref, c):
        return ref.at[c // SUB, pl.ds(pl.multiple_of(lax.rem(c, SUB) * PIECE, PIECE), PIECE), :]

    def move(src, dst, c, send, recv, to):
        return pltpu.make_async_remote_copy(
            src_ref=piece(src, c), dst_ref=piece(dst, c), send_sem=send.at[c], recv_sem=recv.at[c],
            device_id=(to, t, y), device_id_type=MESH,
        )

    def plus(src, c):
        return move(src, rp, c, plus_send, rp_recv, after)

    def minus(src, c):
        return move(src, rm, c, minus_send, rm_recv, before)

    def bminus(src, c):
        return move(src, bm, c, bminus_send, bm_recv, before)

    def bplus(src, c):
        return move(src, bp, c, bplus_send, bp_recv, after)

    def forward(c, _):
        @pl.when(p <= 1)
        def _():
            plus(own, c).start()

        @pl.when(p == 0)
        def _():
            minus(own, c).start()

        @pl.when(p == 2)
        def _():
            plus(own, c).wait_recv()
            piece(fsend, c)[...] = piece(own, c)[...] + carry * piece(rp, c)[...]
            plus(fsend, c).start()

        @pl.when(p == 3)
        def _():
            minus(rm, c).wait_recv()
            minus(rm, c).start()

        return 0

    def forward_rest(c, _):
        @pl.when((p == 1) | (p == 3))
        def _():
            plus(own, c).wait_recv()

        @pl.when(p == 2)
        def _():
            minus(rm, c).wait_recv()

        return 0

    def local_scores(h, _):
        for r in range(2):
            n = HALF * (r + 1)
            at = pl.ds(r * HALF, HALF)
            scores[h, at, pl.ds(0, n)] = (
                mm(take(2, h, r * HALF, HALF), take(0, h, 0, n), 1, 1) * mask[at, pl.ds(0, n)]
            )
        return 0

    def first_half(s, _):
        @pl.when((s == 0) == (p < 2))
        def _():
            lax.fori_loop(0, NC, forward, 0)

        @pl.when((s == 0) != (p < 2))
        def _():
            wait_in(2)
            lax.fori_loop(0, HEADS, local_scores, 0)

        return 0

    lax.fori_loop(0, 2, first_half, 0)
    wait_in(3)

    def attend(h, _):
        lax.fori_loop(h * SUB, h * SUB + SUB, forward_rest, 0)
        state = rp[h] + far_in * rm[h]
        rp[h] = state
        th, tl = split(state)
        at = j * HEADS + h
        gain = gain_ref[pl.ds(at, 1), :]
        gain_part = jnp.zeros((1, DIM), F32)
        state_grad = jnp.zeros((DIM, DIM), F32)
        for r in range(2):
            n = HALF * (r + 1)
            rr = pl.ds(r * HALF, HALF)
            query, value = take(2, h, r * HALF, HALF), take(1, h, 0, n)
            sh, sl = split(scores[h, rr, pl.ds(0, n)])
            used = use[rr, :]
            att = mm(sh, value) + mm(sl, value) + used * (mm(query, th) + mm(query, tl))
            centered = att - jnp.mean(att, axis=-1, keepdims=True)
            inv = lax.rsqrt(jnp.mean(centered * centered, axis=-1, keepdims=True) + EPSILON)
            normed = centered * inv
            up = take(3, h, r * HALF, HALF).astype(F32)
            gain_part = gain_part + jnp.sum(up * normed, axis=0, keepdims=True)
            dn = up * gain
            d_att = inv * (
                dn
                - jnp.mean(dn, axis=-1, keepdims=True)
                - normed * jnp.mean(dn * normed, axis=-1, keepdims=True)
            )
            hi, lo = split(d_att)
            dh[h, rr, :] = hi
            dl[h, rr, :] = lo
            used = used.astype(BF16)
            state_grad = state_grad + mm(query, hi * used, 0, 0) + mm(query, lo * used, 0, 0)
        gsrc[pl.ds(at, 1), :] = gain_part
        sg[h] = state_grad

        @pl.when(p >= 2)
        def _():
            for s in range(SUB):
                bminus(sg, h * SUB + s).start()

        @pl.when(p == 3)
        def _():
            for s in range(SUB):
                bplus(sg, h * SUB + s).start()

        return 0

    lax.fori_loop(0, HEADS, attend, 0)

    gy[y] = gsrc[...]

    def gy_copy(yy):
        return pltpu.make_async_remote_copy(
            src_ref=gy.at[y], dst_ref=gy.at[y], send_sem=gy_send.at[yy], recv_sem=gy_recv.at[y],
            device_id=(z, t, yy), device_id_type=MESH,
        )

    for s in range(1, 4):
        gy_copy(lax.rem(y + s, 4)).start()

    def backward(c, _):
        @pl.when(p == 1)
        def _():
            bminus(sg, c).wait_recv()
            piece(bsend, c)[...] = piece(sg, c)[...] + carry * piece(bm, c)[...]
            bminus(bsend, c).start()

        @pl.when(p == 0)
        def _():
            bplus(bp, c).wait_recv()
            bplus(bp, c).start()

        return 0

    def backward_rest(c, _):
        @pl.when((p == 0) | (p == 2))
        def _():
            bminus(sg, c).wait_recv()

        @pl.when(p == 1)
        def _():
            bplus(bp, c).wait_recv()

        return 0

    def send_out(i):
        def body(s, _):
            g, jj, tt = peer(s)
            pltpu.make_async_remote_copy(
                src_ref=obuf.at[i, pl.ds(pl.multiple_of(g * ROWS, ROWS), ROWS), :],
                dst_ref=out_ref.at[i, :, my_cols],
                send_sem=o_send.at[i],
                recv_sem=o_recv.at[i],
                device_id=(base + jj, tt, y),
                device_id_type=MESH,
            ).start()
            return 0

        lax.fori_loop(1, GROUP, body, 0)
        pltpu.make_async_copy(obuf.at[i, mine, :], out_ref.at[i, :, my_cols], o_recv.at[i]).start()

    def put(i, h, at, value):
        obuf[i, at, pl.ds(pl.multiple_of(h * DIM, DIM), DIM)] = value.astype(BF16)

    def local_grads(h, _):
        th, tl = split(rp[h])
        for r in range(2):
            n = HALF * (r + 1)
            rr, cc = pl.ds(r * HALF, HALF), pl.ds(0, n)
            key, value, query = take(0, h, 0, n), take(1, h, 0, n), take(2, h, r * HALF, HALF)
            hi, lo = dh[h, rr, :], dl[h, rr, :]
            d_sc = (mm(hi, value, 1, 1) + mm(lo, value, 1, 1)) * mask[rr, cc]
            eh, el = split(d_sc)
            sh, sl = split(scores[h, rr, cc])
            d_query = mm(eh, key) + mm(el, key)
            d_query = d_query + use[rr, :] * (mm(hi, th, 1, 1) + mm(hi, tl, 1, 1) + mm(lo, th, 1, 1))
            put(0, h, rr, d_query)
            d_key = mm(eh, query, 0, 0) + mm(el, query, 0, 0)
            d_value = mm(sh, hi, 0, 0) + mm(sl, hi, 0, 0) + mm(sh, lo, 0, 0)
            if r == 0:
                dkl[h, rr, :] = d_key
                dvl[h, rr, :] = d_value
            else:
                low = pl.ds(0, HALF)
                dkl[h, low, :] += d_key[:HALF]
                dvl[h, low, :] += d_value[:HALF]
                dkl[h, rr, :] = d_key[HALF:]
                dvl[h, rr, :] = d_value[HALF:]
        return 0

    def gg_copy(s):
        return pltpu.make_async_remote_copy(
            src_ref=gg.at[j], dst_ref=gg.at[j], send_sem=gg_send.at[s], recv_sem=gg_recv.at[j],
            device_id=(base + lax.rem(j + s, GZ), t, y), device_id_type=MESH,
        )

    def second_half(s, _):
        @pl.when((s == 0) == (p <= 1))
        def _():
            lax.fori_loop(0, HEADS, local_grads, 0)
            send_out(0)

        @pl.when((s == 0) != (p <= 1))
        def _():
            lax.fori_loop(0, NC, backward, 0)

        return 0

    lax.fori_loop(0, 2, second_half, 0)

    for s in range(1, 4):
        yy = lax.rem(y + s, 4)
        pltpu.make_async_copy(gy.at[yy], gy.at[yy], gy_recv.at[yy]).wait()
    gg[j] = (gy[0] + gy[1]) + (gy[2] + gy[3])
    for s in range(1, GZ):
        gg_copy(s).start()

    def last_grads(h, _):
        lax.fori_loop(h * SUB, h * SUB + SUB, backward_rest, 0)
        gh, gl = split(bm[h] + far_out * bp[h])
        key, value = take(0, h), take(1, h)
        everything = pl.ds(0, TOK)
        put(1, h, everything, dkl[h] + keep[...] * (mm(value, gh, 1, 1) + mm(value, gl, 1, 1)))
        put(2, h, everything, dvl[h] + keep[...] * (mm(key, gh) + mm(key, gl)))
        return 0

    lax.fori_loop(0, HEADS, last_grads, 0)
    send_out(1)
    send_out(2)

    for s in range(1, GZ):
        jj = lax.rem(j + s, GZ)
        pltpu.make_async_copy(gg.at[jj], gg.at[jj], gg_recv.at[jj]).wait()
    gz[0] = (gg[0] + gg[1]) + (gg[2] + gg[3])

    def gz_copy(i, partner):
        return pltpu.make_async_remote_copy(
            src_ref=gz.at[2 * i], dst_ref=gz.at[2 * i + 1], send_sem=gz_send.at[i], recv_sem=gz_recv.at[i],
            device_id=(partner, t, y), device_id_type=MESH,
        )

    even = lax.rem(p, 2) == 0
    near = jnp.where(even, after, before)
    other = jnp.where(even, before, after)
    gz_copy(0, near).start()
    gz_copy(0, near).wait_recv()
    gz[2] = gz[0] + gz[1]
    gz_copy(1, other).start()
    gz_copy(1, other).wait_recv()
    gout_ref[...] = (gz[2] + gz[3]) / math.sqrt(4 * SEQ * 128)

    for i in range(3):
        pltpu.make_async_copy(out_ref.at[i], out_ref.at[i], o_recv.at[i]).wait()
    for a in range(4):
        part = buf.at[a, pl.ds(0, TOK - ROWS), :]
        pltpu.make_async_copy(part, part, in_send.at[a]).wait()
    for i in range(3):
        part = obuf.at[i, pl.ds(0, TOK - ROWS), :]
        pltpu.make_async_copy(part, part, o_send.at[i]).wait()
    gz_copy(0, near).wait_send()
    gz_copy(1, other).wait_send()
    for s in range(1, GZ):
        gg_copy(s).wait_send()
    for s in range(1, 4):
        gy_copy(lax.rem(y + s, 4)).wait_send()

    def drain(c, _):
        @pl.when(p <= 2)
        def _():
            plus(own, c).wait_send()

        @pl.when((p == 0) | (p == 3))
        def _():
            minus(own, c).wait_send()
            bplus(sg, c).wait_send()

        @pl.when(p >= 1)
        def _():
            bminus(sg, c).wait_send()

        return 0

    lax.fori_loop(0, NC, drain, 0)


def place(grads_ref, gain_ref, q_ref, k_ref, v_ref, g_ref, sems):
    copies = [
        pltpu.make_async_copy(grads_ref.at[i], ref.at[0], sems.at[i])
        for i, ref in enumerate((q_ref, k_ref, v_ref))
    ]
    for copy in copies:
        copy.start()
    g_ref[...] = gain_ref[...]
    for copy in copies:
        copy.wait()


def local(query_rows, key_rows, value_rows, cotangent, norm_gain, doc_starts):
    anywhere = pl.BlockSpec(memory_space=pl.ANY)
    hbm = pl.BlockSpec(memory_space=pltpu.HBM)
    vmem = pl.BlockSpec(memory_space=pltpu.VMEM)
    smem = pl.BlockSpec(memory_space=pltpu.SMEM)
    dma = pltpu.SemaphoreType.DMA
    state = pltpu.VMEM((HEADS, DIM, DIM), F32)
    grads, gain_sum = pl.pallas_call(
        kernel,
        out_shape=(
            jax.ShapeDtypeStruct((3, ROWS, 8192), BF16),
            jax.ShapeDtypeStruct((8, DIM), F32),
        ),
        in_specs=[hbm] * 4 + [vmem, smem],
        out_specs=(anywhere, vmem),
        scratch_shapes=[
            pltpu.VMEM((4, TOK, COLS), BF16),
            pltpu.VMEM((TOK, TOK), F32),
            pltpu.VMEM((TOK, DIM), F32),
            pltpu.VMEM((TOK, DIM), F32),
            state, state, state, state, state, state, state, state,
            pltpu.VMEM((HEADS, TOK, TOK), F32),
            pltpu.VMEM((HEADS, TOK, DIM), BF16),
            pltpu.VMEM((HEADS, TOK, DIM), BF16),
            pltpu.VMEM((HEADS, TOK, DIM), F32),
            pltpu.VMEM((HEADS, TOK, DIM), F32),
            pltpu.VMEM((3, TOK, COLS), BF16),
            pltpu.VMEM((8, DIM), F32),
            pltpu.VMEM((4, 8, DIM), F32),
            pltpu.VMEM((GZ, 8, DIM), F32),
            pltpu.VMEM((4, 8, DIM), F32),
            dma((4,)), dma((4,)),
            dma((NC,)), dma((NC,)), dma((NC,)), dma((NC,)), dma((NC,)), dma((NC,)), dma((NC,)), dma((NC,)),
            dma((3,)), dma((3,)), dma((4,)), dma((4,)), dma((GZ,)), dma((GZ,)), dma((2,)), dma((2,)),
        ],
        compiler_params=pltpu.CompilerParams(
            collective_id=1, has_side_effects=True, vmem_limit_bytes=60 * 1024 * 1024
        ),
        name="layer",
    )(key_rows, value_rows, query_rows, cotangent, norm_gain.reshape(8, DIM), doc_starts)
    rows = jax.ShapeDtypeStruct((1, ROWS, 8192), BF16)
    grad_q, grad_k, grad_v, gain = pl.pallas_call(
        place,
        out_shape=(rows, rows, rows, jax.ShapeDtypeStruct((8, DIM), F32)),
        in_specs=[vmem, vmem],
        out_specs=(anywhere, anywhere, anywhere, vmem),
        scratch_shapes=[dma((3,))],
        name="place",
    )(grads, gain_sum)
    return grad_q, grad_k, grad_v, gain.reshape(8 * DIM)


def solution(mesh):
    rows = P("dp", ("seq", "tensor"), None)
    return jax.shard_map(
        local,
        mesh=mesh,
        in_specs=(rows, rows, rows, rows, P("tensor"), P("dp", None)),
        out_specs=(rows, rows, rows, P("tensor")),
        check_vma=False,
    )
```

```python
import functools
import math

import jax
import jax.numpy as jnp
from jax import lax
from jax.experimental import pallas as pl
from jax.experimental.pallas import tpu as pltpu
from jax.sharding import PartitionSpec as P

MESH = pl.DeviceIdType.MESH
F32 = jnp.float32
BF16 = jnp.bfloat16
EPSILON = 1e-05
DIM = 128
HEADS = 2
GZ = 4
POS = 4
TOK = 512
HALF = 256
COLS = HEADS * DIM
ROWS = 16
GROUP = 32
SEQ = 16
CODED = DIM + 16


def split(x):
    hi = x.astype(BF16)
    return hi, (x - hi.astype(F32)).astype(BF16)


def encode(x):
    top = jnp.maximum(jnp.max(jnp.abs(x), axis=0, keepdims=True), 1e-30)
    power = jnp.floor(jnp.log(top) * (1 / math.log(2)))
    coded = jnp.clip(jnp.floor(x * jnp.exp2(14 - power) + 0.5), -32767, 32767)
    rows = jnp.concatenate([coded, jnp.broadcast_to(power, (CODED - DIM, DIM))], axis=0)
    return rows.astype(jnp.int32).astype(jnp.int16)


def decode(coded):
    values = coded.astype(jnp.int32).astype(F32)
    return values[:DIM] * jnp.exp2(values[DIM : DIM + 1] - 14)


def mm(a, b, ca=1, cb=0):
    return lax.dot_general(a, b, (((ca,), (cb,)), ((), ())), preferred_element_type=F32)


def kernel(
    k_ref, v_ref, q_ref, c_ref, gain_ref, starts_ref,
    out_ref, gout_ref,
    stage, kv, qc, mask, use, keep, own, own_c, fsend, rp, rm, states, sg, sg_c, bsend, bm, bp, scores, dh, dl, dkl, dvl, dq, dkv,
    gsrc, gy, gg, gz,
    st_sem, kv_send, kv_recv, qc_send, qc_recv,
    plus_send, rp_recv, minus_send, rm_recv, bminus_send, bm_recv, bplus_send, bp_recv,
    dq_send, dq_recv, dkv_send, dkv_recv, gy_send, gy_recv, gg_send, gg_recv, gz_send, gz_recv, ready, ready_y,
):
    z, t, y = lax.axis_index("seq"), lax.axis_index("tensor"), lax.axis_index("dp")
    p, j = z // GZ, lax.rem(z, GZ)
    base = p * GZ
    me = j * 8 + t
    after, before = lax.rem(z + GZ, SEQ), lax.rem(z + SEQ - GZ, SEQ)

    def peer(s):
        g = lax.rem(me + s, GROUP)
        return g, g // 8, lax.rem(g, 8)

    def staged(a, ref):
        return pltpu.make_async_copy(ref.at[0], stage.at[a], st_sem.at[a])

    rows_in = ((0, k_ref), (1, v_ref), (2, q_ref), (3, c_ref))
    for a, ref in rows_in:
        staged(a, ref).start()

    barrier = pltpu.get_barrier_semaphore()

    def greet(zz, tt, yy):
        pl.semaphore_signal(barrier, inc=1, device_id=(zz, tt, yy), device_id_type=MESH)

    @pl.when(p < POS - 1)
    def _():
        greet(after, t, y)

    @pl.when(p == 0)
    def _():
        greet(before, t, y)

    for yy in range(1, 4):
        @pl.when(yy > y)
        def _():
            greet(z, t, yy)

    def greet_group(s, _):
        _, jj, tt = peer(s)
        greet(base + jj, tt, y)
        return 0

    lax.fori_loop(1, GROUP, greet_group, 0)

    def count(tok):
        total = jnp.zeros_like(tok)
        for i in range(8):
            total = total + (starts_ref[0, i] <= tok).astype(jnp.int32)
        return total

    first = base * 128
    prev = count(first - 1)
    last = count(first + TOK - 1)
    carry = (prev == last).astype(F32)
    far_in = (count(TOK - 1) == prev).astype(F32)
    far_out = (last == count(3 * TOK - 1)).astype(F32)
    row = lax.broadcasted_iota(jnp.int32, (TOK, DIM), 0) + first
    seg = count(row)
    use[...] = (seg == prev).astype(F32)
    keep[...] = (seg == last).astype(F32)
    seg_row = count(lax.broadcasted_iota(jnp.int32, (8, TOK), 1) + first)[:1]
    seg_col = jnp.concatenate([seg] * 4, axis=1)
    rows = lax.broadcasted_iota(jnp.int32, (TOK, TOK), 0)
    cols = lax.broadcasted_iota(jnp.int32, (TOK, TOK), 1)
    mask[...] = ((rows >= cols) & (seg_col == seg_row)).astype(F32)
    gsrc[...] = jnp.zeros_like(gsrc)

    @pl.when(p == 0)
    def _():
        rp[...] = jnp.zeros_like(rp)

    @pl.when(p <= 1)
    def _():
        rm[...] = jnp.zeros_like(rm)

    @pl.when(p == 3)
    def _():
        bm[...] = jnp.zeros_like(bm)

    @pl.when(p >= 2)
    def _():
        bp[...] = jnp.zeros_like(bp)

    pl.semaphore_wait(barrier, 31 + y + (p + 1) // 2)

    def answer(sem, zz, yy):
        pl.semaphore_signal(sem, inc=1, device_id=(zz, t, yy), device_id_type=MESH)

    @pl.when(p > 0)
    def _():
        answer(ready.at[0], before, y)

    @pl.when(p == POS - 1)
    def _():
        answer(ready.at[1], after, y)

    for yy in range(3):
        @pl.when(yy < y)
        def _():
            answer(ready_y.at[y], z, yy)

    mine = pl.ds(pl.multiple_of(me * ROWS, ROWS), ROWS)
    my_cols = pl.ds(pl.multiple_of(t * 1024 + j * COLS, COLS), COLS)

    def to_heads(src, dst, jj, tt, send, recv):
        return pltpu.make_async_remote_copy(
            src_ref=src, dst_ref=dst, send_sem=send, recv_sem=recv,
            device_id=(base + jj, tt, y), device_id_type=MESH,
        )

    def send_kv(s, _):
        g, jj, tt = peer(s)
        at = pl.ds(pl.multiple_of(tt * 1024 + jj * COLS, COLS), COLS)
        to_heads(stage.at[pl.ds(0, 2), :, at], kv.at[:, mine, :], jj, tt, kv_send, kv_recv).start()
        return 0

    def send_qc(h):
        def body(s, _):
            g, jj, tt = peer(s)
            at = pl.ds(pl.multiple_of(tt * 1024 + jj * COLS + h * DIM, DIM), DIM)
            to_heads(
                stage.at[pl.ds(2, 2), :, at], qc.at[h, :, mine, :], jj, tt, qc_send.at[h], qc_recv.at[h]
            ).start()
            return 0

        lax.fori_loop(1, GROUP, body, 0)
        at = pl.ds(pl.multiple_of(t * 1024 + j * COLS + h * DIM, DIM), DIM)
        pltpu.make_async_copy(stage.at[pl.ds(2, 2), :, at], qc.at[h, :, mine, :], qc_recv.at[h]).start()

    staged(0, k_ref).wait()
    staged(1, v_ref).wait()
    lax.fori_loop(1, GROUP, send_kv, 0)
    pltpu.make_async_copy(stage.at[pl.ds(0, 2), :, my_cols], kv.at[:, mine, :], kv_recv).start()
    def take(a, h, start=0, size=TOK):
        if a < 2:
            return kv[a, pl.ds(start, size), pl.ds(pl.multiple_of(h * DIM, DIM), DIM)]
        return qc[h, a - 2, pl.ds(start, size), :]

    staged(2, q_ref).wait()
    staged(3, c_ref).wait()
    for h in range(HEADS):
        send_qc(h)
    pltpu.make_async_copy(kv, kv, kv_recv).wait()

    def local_state(h, _):
        kept = take(0, h) * keep[...].astype(BF16)
        own[h] = mm(kept, take(1, h), 0, 0)
        own_c[h] = encode(own[h])
        return 0

    lax.fori_loop(0, HEADS, local_state, 0)

    def move(src, dst, c, send, recv, to):
        return pltpu.make_async_remote_copy(
            src_ref=src.at[c], dst_ref=dst.at[c], send_sem=send.at[c], recv_sem=recv.at[c],
            device_id=(to, t, y), device_id_type=MESH,
        )

    def plus(src, c):
        return move(src, rp, c, plus_send, rp_recv, after)

    def minus(src, c):
        return move(src, rm, c, minus_send, rm_recv, before)

    def bminus(src, c):
        return move(src, bm, c, bminus_send, bm_recv, before)

    def bplus(src, c):
        return move(src, bp, c, bplus_send, bp_recv, after)

    def forward(c, _):
        @pl.when(p <= 1)
        def _():
            plus(own_c, c).start()

        @pl.when(p == 0)
        def _():
            minus(own_c, c).start()

        @pl.when(p == 2)
        def _():
            plus(own_c, c).wait_recv()
            fsend[c] = encode(own[c] + carry * decode(rp[c]))
            plus(fsend, c).start()

        @pl.when(p == 3)
        def _():
            minus(rm, c).wait_recv()
            minus(rm, c).start()

        return 0

    def forward_rest(c, _):
        @pl.when((p == 1) | (p == 3))
        def _():
            plus(own_c, c).wait_recv()

        @pl.when(p == 2)
        def _():
            minus(rm, c).wait_recv()

        return 0

    def local_scores(h, _):
        for r in range(2):
            n = HALF * (r + 1)
            at = pl.ds(r * HALF, HALF)
            scores[h, at, pl.ds(0, n)] = (
                mm(take(2, h, r * HALF, HALF), take(0, h, 0, n), 1, 1) * mask[at, pl.ds(0, n)]
            )
        return 0

    @pl.when(p < POS - 1)
    def _():
        pl.semaphore_wait(ready.at[0], 1)

    @pl.when(p == 0)
    def _():
        pl.semaphore_wait(ready.at[1], 1)

    lax.fori_loop(0, HEADS, forward, 0)

    def attend(h, _):
        pltpu.make_async_copy(qc.at[h], qc.at[h], qc_recv.at[h]).wait()
        local_scores(h, 0)
        forward_rest(h, 0)
        state = decode(rp[h]) + far_in * decode(rm[h])
        states[h] = state
        th, tl = split(state)
        at = j * HEADS + h
        gain = gain_ref[pl.ds(at, 1), :]
        gain_part = jnp.zeros((1, DIM), F32)
        state_grad = jnp.zeros((DIM, DIM), F32)
        for r in range(2):
            n = HALF * (r + 1)
            rr = pl.ds(r * HALF, HALF)
            query, value = take(2, h, r * HALF, HALF), take(1, h, 0, n)
            sh, sl = split(scores[h, rr, pl.ds(0, n)])
            used = use[rr, :]
            att = mm(sh, value) + mm(sl, value) + used * (mm(query, th) + mm(query, tl))
            centered = att - jnp.mean(att, axis=-1, keepdims=True)
            inv = lax.rsqrt(jnp.mean(centered * centered, axis=-1, keepdims=True) + EPSILON)
            normed = centered * inv
            up = take(3, h, r * HALF, HALF).astype(F32)
            gain_part = gain_part + jnp.sum(up * normed, axis=0, keepdims=True)
            dn = up * gain
            d_att = inv * (
                dn
                - jnp.mean(dn, axis=-1, keepdims=True)
                - normed * jnp.mean(dn * normed, axis=-1, keepdims=True)
            )
            hi, lo = split(d_att)
            dh[h, rr, :] = hi
            dl[h, rr, :] = lo
            used = used.astype(BF16)
            state_grad = state_grad + mm(query, hi * used, 0, 0) + mm(query, lo * used, 0, 0)
        gsrc[pl.ds(at, 1), :] = gain_part
        sg[h] = state_grad
        sg_c[h] = encode(state_grad)

        @pl.when(p >= 2)
        def _():
            bminus(sg_c, h).start()

        @pl.when(p == 3)
        def _():
            bplus(sg_c, h).start()

        return 0

    lax.fori_loop(0, HEADS, attend, 0)

    gy[y] = gsrc[...]

    def gy_copy(yy):
        return pltpu.make_async_remote_copy(
            src_ref=gy.at[y], dst_ref=gy.at[y], send_sem=gy_send.at[yy], recv_sem=gy_recv.at[y],
            device_id=(z, t, yy), device_id_type=MESH,
        )

    for yy in range(1, 4):
        @pl.when(yy > y)
        def _():
            pl.semaphore_wait(ready_y.at[yy], 1)

    for s in range(1, 4):
        gy_copy(lax.rem(y + s, 4)).start()

    def backward(c, _):
        @pl.when(p == 1)
        def _():
            bminus(sg_c, c).wait_recv()
            bsend[c] = encode(sg[c] + carry * decode(bm[c]))
            bminus(bsend, c).start()

        @pl.when(p == 0)
        def _():
            bplus(bp, c).wait_recv()
            bplus(bp, c).start()

        return 0

    def backward_rest(c, _):
        @pl.when((p == 0) | (p == 2))
        def _():
            bminus(sg_c, c).wait_recv()

        @pl.when(p == 1)
        def _():
            bplus(bp, c).wait_recv()

        return 0

    def send_dq(s, _):
        g, jj, tt = peer(s)
        at = pl.ds(pl.multiple_of(g * ROWS, ROWS), ROWS)
        to_heads(dq.at[at, :], out_ref.at[0, :, my_cols], jj, tt, dq_send, dq_recv).start()
        return 0

    def send_dkv(h):
        cols = pl.ds(pl.multiple_of(t * 1024 + j * COLS + h * DIM, DIM), DIM)

        def body(s, _):
            g, jj, tt = peer(s)
            at = pl.ds(pl.multiple_of(g * ROWS, ROWS), ROWS)
            to_heads(
                dkv.at[h, :, at, :], out_ref.at[pl.ds(1, 2), :, cols], jj, tt, dkv_send.at[h], dkv_recv.at[h]
            ).start()
            return 0

        lax.fori_loop(1, GROUP, body, 0)
        pltpu.make_async_copy(dkv.at[h, :, mine, :], out_ref.at[pl.ds(1, 2), :, cols], dkv_recv.at[h]).start()

    def local_grads(h, _):
        th, tl = split(states[h])
        for r in range(2):
            n = HALF * (r + 1)
            rr, cc = pl.ds(r * HALF, HALF), pl.ds(0, n)
            key, value, query = take(0, h, 0, n), take(1, h, 0, n), take(2, h, r * HALF, HALF)
            hi, lo = dh[h, rr, :], dl[h, rr, :]
            d_sc = (mm(hi, value, 1, 1) + mm(lo, value, 1, 1)) * mask[rr, cc]
            eh, el = split(d_sc)
            sh, sl = split(scores[h, rr, cc])
            d_query = mm(eh, key) + mm(el, key)
            d_query = d_query + use[rr, :] * (mm(hi, th, 1, 1) + mm(hi, tl, 1, 1) + mm(lo, th, 1, 1))
            dq[rr, pl.ds(pl.multiple_of(h * DIM, DIM), DIM)] = d_query.astype(BF16)
            d_key = mm(eh, query, 0, 0) + mm(el, query, 0, 0)
            d_value = mm(sh, hi, 0, 0) + mm(sl, hi, 0, 0) + mm(sh, lo, 0, 0)
            if r == 0:
                dkl[h, rr, :] = d_key
                dvl[h, rr, :] = d_value
            else:
                low = pl.ds(0, HALF)
                dkl[h, low, :] += d_key[:HALF]
                dvl[h, low, :] += d_value[:HALF]
                dkl[h, rr, :] = d_key[HALF:]
                dvl[h, rr, :] = d_value[HALF:]
        return 0

    def gg_copy(s):
        return pltpu.make_async_remote_copy(
            src_ref=gg.at[j], dst_ref=gg.at[j], send_sem=gg_send.at[s], recv_sem=gg_recv.at[j],
            device_id=(base + lax.rem(j + s, GZ), t, y), device_id_type=MESH,
        )

    lax.fori_loop(0, HEADS, local_grads, 0)
    lax.fori_loop(1, GROUP, send_dq, 0)
    pltpu.make_async_copy(dq.at[mine, :], out_ref.at[0, :, my_cols], dq_recv).start()

    for s in range(1, 4):
        yy = lax.rem(y + s, 4)
        pltpu.make_async_copy(gy.at[yy], gy.at[yy], gy_recv.at[yy]).wait()
    gg[j] = (gy[0] + gy[1]) + (gy[2] + gy[3])
    for s in range(1, GZ):
        gg_copy(s).start()

    lax.fori_loop(0, HEADS, backward, 0)

    even = lax.rem(p, 2) == 0
    near = jnp.where(even, after, before)
    other = jnp.where(even, before, after)

    def gz_copy(i, partner):
        return pltpu.make_async_remote_copy(
            src_ref=gz.at[2 * i], dst_ref=gz.at[2 * i + 1], send_sem=gz_send.at[i], recv_sem=gz_recv.at[i],
            device_id=(partner, t, y), device_id_type=MESH,
        )

    def last_grads(h, _):
        backward_rest(h, 0)
        gh, gl = split(decode(bm[h]) + far_out * decode(bp[h]))
        key, value = take(0, h), take(1, h)
        d_key = dkl[h] + keep[...] * (mm(value, gh, 1, 1) + mm(value, gl, 1, 1))
        d_value = dvl[h] + keep[...] * (mm(key, gh) + mm(key, gl))
        dkv[h, 0] = d_key.astype(BF16)
        dkv[h, 1] = d_value.astype(BF16)
        send_dkv(h)

        @pl.when(h == 0)
        def _():
            for s in range(1, GZ):
                jj = lax.rem(j + s, GZ)
                pltpu.make_async_copy(gg.at[jj], gg.at[jj], gg_recv.at[jj]).wait()
            gz[0] = (gg[0] + gg[1]) + (gg[2] + gg[3])
            gz_copy(0, near).start()

        return 0

    lax.fori_loop(0, HEADS, last_grads, 0)
    gz_copy(0, near).wait_recv()
    gz[2] = gz[0] + gz[1]
    gz_copy(1, other).start()
    gz_copy(1, other).wait_recv()
    gout_ref[...] = (gz[2] + gz[3]) / math.sqrt(4 * SEQ * 128)

    pltpu.make_async_copy(out_ref.at[0], out_ref.at[0], dq_recv).wait()
    for h in range(HEADS):
        pltpu.make_async_copy(out_ref.at[1 + h], out_ref.at[1 + h], dkv_recv.at[h]).wait()
    most = pl.ds(0, TOK - ROWS)
    pltpu.make_async_copy(kv.at[:, most, :], kv.at[:, most, :], kv_send).wait()
    pltpu.make_async_copy(dq.at[most, :], dq.at[most, :], dq_send).wait()
    for h in range(HEADS):
        pltpu.make_async_copy(qc.at[h, :, most, :], qc.at[h, :, most, :], qc_send.at[h]).wait()
        pltpu.make_async_copy(dkv.at[h, :, most, :], dkv.at[h, :, most, :], dkv_send.at[h]).wait()
    gz_copy(0, near).wait_send()
    gz_copy(1, other).wait_send()
    for s in range(1, GZ):
        gg_copy(s).wait_send()
    for s in range(1, 4):
        gy_copy(lax.rem(y + s, 4)).wait_send()

    def drain(c, _):
        @pl.when(p <= 2)
        def _():
            plus(own_c, c).wait_send()

        @pl.when((p == 0) | (p == 3))
        def _():
            minus(own_c, c).wait_send()
            bplus(sg_c, c).wait_send()

        @pl.when(p >= 1)
        def _():
            bminus(sg_c, c).wait_send()

        return 0

    lax.fori_loop(0, HEADS, drain, 0)


def place(grads_ref, gain_ref, q_ref, k_ref, v_ref, g_ref, sems):
    copies = [
        pltpu.make_async_copy(grads_ref.at[i], ref.at[0], sems.at[i])
        for i, ref in enumerate((q_ref, k_ref, v_ref))
    ]
    for copy in copies:
        copy.start()
    g_ref[...] = gain_ref[...]
    for copy in copies:
        copy.wait()


def local(query_rows, key_rows, value_rows, cotangent, norm_gain, doc_starts):
    anywhere = pl.BlockSpec(memory_space=pl.ANY)
    hbm = pl.BlockSpec(memory_space=pltpu.HBM)
    vmem = pl.BlockSpec(memory_space=pltpu.VMEM)
    smem = pl.BlockSpec(memory_space=pltpu.SMEM)
    dma = pltpu.SemaphoreType.DMA
    state = pltpu.VMEM((HEADS, DIM, DIM), F32)
    coded = pltpu.VMEM((HEADS, CODED, DIM), jnp.int16)
    grads, gain_sum = pl.pallas_call(
        kernel,
        out_shape=(
            jax.ShapeDtypeStruct((3, ROWS, 8192), BF16),
            jax.ShapeDtypeStruct((8, DIM), F32),
        ),
        in_specs=[hbm] * 4 + [vmem, smem],
        out_specs=(anywhere, vmem),
        scratch_shapes=[
            pltpu.VMEM((4, ROWS, 8192), BF16),
            pltpu.VMEM((2, TOK, COLS), BF16),
            pltpu.VMEM((HEADS, 2, TOK, DIM), BF16),
            pltpu.VMEM((TOK, TOK), F32),
            pltpu.VMEM((TOK, DIM), F32),
            pltpu.VMEM((TOK, DIM), F32),
            state, coded, coded, coded, coded, state, state, coded, coded, coded, coded,
            pltpu.VMEM((HEADS, TOK, TOK), F32),
            pltpu.VMEM((HEADS, TOK, DIM), BF16),
            pltpu.VMEM((HEADS, TOK, DIM), BF16),
            pltpu.VMEM((HEADS, TOK, DIM), F32),
            pltpu.VMEM((HEADS, TOK, DIM), F32),
            pltpu.VMEM((TOK, COLS), BF16),
            pltpu.VMEM((HEADS, 2, TOK, DIM), BF16),
            pltpu.VMEM((8, DIM), F32),
            pltpu.VMEM((4, 8, DIM), F32),
            pltpu.VMEM((GZ, 8, DIM), F32),
            pltpu.VMEM((4, 8, DIM), F32),
            dma((4,)), dma, dma, dma((HEADS,)), dma((HEADS,)),
            dma((HEADS,)), dma((HEADS,)), dma((HEADS,)), dma((HEADS,)),
            dma((HEADS,)), dma((HEADS,)), dma((HEADS,)), dma((HEADS,)),
            dma, dma, dma((HEADS,)), dma((HEADS,)),
            dma((4,)), dma((4,)), dma((GZ,)), dma((GZ,)), dma((2,)), dma((2,)),
            pltpu.SemaphoreType.REGULAR((2,)), pltpu.SemaphoreType.REGULAR((4,)),
        ],
        compiler_params=pltpu.CompilerParams(
            collective_id=1, has_side_effects=True, vmem_limit_bytes=60 * 1024 * 1024
        ),
        name="layer",
    )(key_rows, value_rows, query_rows, cotangent, norm_gain.reshape(8, DIM), doc_starts)
    rows = jax.ShapeDtypeStruct((1, ROWS, 8192), BF16)
    grad_q, grad_k, grad_v, gain = pl.pallas_call(
        place,
        out_shape=(rows, rows, rows, jax.ShapeDtypeStruct((8, DIM), F32)),
        in_specs=[vmem, vmem],
        out_specs=(anywhere, anywhere, anywhere, vmem),
        scratch_shapes=[dma((3,))],
        name="place",
    )(grads, gain_sum)
    return grad_q, grad_k, grad_v, gain.reshape(8 * DIM)


def solution(mesh):
    rows = P("dp", ("seq", "tensor"), None)
    return jax.shard_map(
        local,
        mesh=mesh,
        in_specs=(rows, rows, rows, rows, P("tensor"), P("dp", None)),
        out_specs=(rows, rows, rows, P("tensor")),
        check_vma=False,
    )
```

```python
import functools
import math

import jax
import jax.numpy as jnp
from jax import lax
from jax.experimental import pallas as pl
from jax.experimental.pallas import tpu as pltpu
from jax.sharding import PartitionSpec as P

MESH = pl.DeviceIdType.MESH
F32 = jnp.float32
BF16 = jnp.bfloat16
EPSILON = 1e-05
DIM = 128
HEADS = 2
GZ = 4
POS = 4
TOK = 512
HALF = 256
COLS = HEADS * DIM
ROWS = 16
GROUP = 32
SEQ = 16
CODED = DIM + 16


def split(x):
    hi = x.astype(BF16)
    return hi, (x - hi.astype(F32)).astype(BF16)


def encode(x):
    top = jnp.maximum(jnp.max(jnp.abs(x), axis=0, keepdims=True), 1e-30)
    power = jnp.floor(jnp.log(top) * (1 / math.log(2)))
    coded = jnp.clip(jnp.floor(x * jnp.exp2(14 - power) + 0.5), -32767, 32767)
    rows = jnp.concatenate([coded, jnp.broadcast_to(power, (CODED - DIM, DIM))], axis=0)
    return rows.astype(jnp.int32).astype(jnp.int16)


def decode(coded):
    values = coded.astype(jnp.int32).astype(F32)
    return values[:DIM] * jnp.exp2(values[DIM : DIM + 1] - 14)


def mm(a, b, ca=1, cb=0):
    return lax.dot_general(a, b, (((ca,), (cb,)), ((), ())), preferred_element_type=F32)


def kernel(
    k_ref, v_ref, q_ref, c_ref, gain_in, starts_in,
    out_ref, gout_ref,
    stage, kv, qc, mask, use, keep, own, own_c, fsend, rp, rm, states, sg_c, b1, b2, b3, inner, scores, dh, dl, dkl, dvl, dq, dkv,
    gsrc, gy, gg, gz,
    st_sem, kv_send, kv_recv, qc_send, qc_recv,
    plus_send, rp_recv, minus_send, rm_recv, b1_send, b1_recv, b2_send, b2_recv, b3_send, b3_recv,
    dq_send, dq_recv, dkv_send, dkv_recv, gy_send, gy_recv, gg_send, gg_recv, gz_send, gz_recv, ready, ready_y, gain_ref, starts_ref, small_sem,
):
    z, t, y = lax.axis_index("seq"), lax.axis_index("tensor"), lax.axis_index("dp")
    p, j = z // GZ, lax.rem(z, GZ)
    base = p * GZ
    me = j * 8 + t
    after, before = lax.rem(z + GZ, SEQ), lax.rem(z + SEQ - GZ, SEQ)

    def peer(s):
        g = lax.rem(me + s, GROUP)
        return g, g // 8, lax.rem(g, 8)

    def staged(a, ref):
        return pltpu.make_async_copy(ref.at[0], stage.at[a], st_sem.at[a])

    rows_in = ((0, k_ref), (1, v_ref), (2, q_ref), (3, c_ref))
    for a, ref in rows_in:
        staged(a, ref).start()

    small = (
        pltpu.make_async_copy(gain_in, gain_ref, small_sem.at[0]),
        pltpu.make_async_copy(starts_in, starts_ref, small_sem.at[1]),
    )
    for copy in small:
        copy.start()

    barrier = pltpu.get_barrier_semaphore()

    def greet(zz, tt, yy):
        pl.semaphore_signal(barrier, inc=1, device_id=(zz, tt, yy), device_id_type=MESH)

    for d in range(1, POS):
        @pl.when(p + d < POS)
        def _():
            greet(lax.rem(z + d * GZ, SEQ), t, y)

    for yy in range(1, 4):
        @pl.when(yy > y)
        def _():
            greet(z, t, yy)

    def greet_group(s, _):
        _, jj, tt = peer(s)
        greet(base + jj, tt, y)
        return 0

    lax.fori_loop(1, GROUP, greet_group, 0)

    pl.semaphore_wait(barrier, 31 + y + p)

    def answer(sem, zz, yy):
        pl.semaphore_signal(sem, inc=1, device_id=(zz, t, yy), device_id_type=MESH)

    @pl.when(p > 0)
    def _():
        answer(ready.at[0], before, y)

    @pl.when(p == POS - 1)
    def _():
        answer(ready.at[1], after, y)

    for yy in range(3):
        @pl.when(yy < y)
        def _():
            answer(ready_y.at[y], z, yy)

    mine = pl.ds(pl.multiple_of(me * ROWS, ROWS), ROWS)
    my_cols = pl.ds(pl.multiple_of(t * 1024 + j * COLS, COLS), COLS)

    def to_heads(src, dst, jj, tt, send, recv):
        return pltpu.make_async_remote_copy(
            src_ref=src, dst_ref=dst, send_sem=send, recv_sem=recv,
            device_id=(base + jj, tt, y), device_id_type=MESH,
        )

    def send_in(first_row, dst, send, recv, h):
        def part(tt, jj):
            cols = pl.ds(pl.multiple_of(tt * 1024 + jj * COLS + h * DIM, DIM), DIM)
            return stage.at[pl.ds(first_row, 2), :, cols]

        def body(s, _):
            g, jj, tt = peer(s)
            to_heads(part(tt, jj), dst.at[h, :, mine, :], jj, tt, send.at[h], recv.at[h]).start()
            return 0

        lax.fori_loop(1, GROUP, body, 0)
        pltpu.make_async_copy(part(t, j), dst.at[h, :, mine, :], recv.at[h]).start()

    def send_kv(h):
        send_in(0, kv, kv_send, kv_recv, h)

    def send_qc(h):
        send_in(2, qc, qc_send, qc_recv, h)

    staged(0, k_ref).wait()
    staged(1, v_ref).wait()
    send_kv(0)
    staged(2, q_ref).wait()
    staged(3, c_ref).wait()

    @pl.when(p >= 2)
    def _():
        send_qc(0)

    def take(a, h, start=0, size=TOK):
        if a < 2:
            return kv[h, a, pl.ds(start, size), :]
        return qc[h, a - 2, pl.ds(start, size), :]

    def count(tok):
        total = jnp.zeros_like(tok)
        for i in range(8):
            total = total + (starts_ref[0, i] <= tok).astype(jnp.int32)
        return total

    for copy in small:
        copy.wait()
    first = base * 128
    prev = count(first - 1)
    last = count(first + TOK - 1)
    carry = (prev == last).astype(F32)
    far_in = (count(TOK - 1) == prev).astype(F32)
    out2 = (last == count(first + 2 * TOK - 1)).astype(F32)
    out3 = (last == count(first + 3 * TOK - 1)).astype(F32)
    row = lax.broadcasted_iota(jnp.int32, (TOK, DIM), 0) + first
    seg = count(row)
    use[...] = (seg == prev).astype(F32)
    keep[...] = (seg == last).astype(F32)
    seg_row = count(lax.broadcasted_iota(jnp.int32, (8, TOK), 1) + first)[:1]
    seg_col = jnp.concatenate([seg] * 4, axis=1)
    rows = lax.broadcasted_iota(jnp.int32, (TOK, TOK), 0)
    cols = lax.broadcasted_iota(jnp.int32, (TOK, TOK), 1)
    mask[...] = ((rows >= cols) & (seg_col == seg_row)).astype(F32)
    gsrc[...] = jnp.zeros_like(gsrc)

    @pl.when(p == 0)
    def _():
        rp[...] = jnp.zeros_like(rp)

    @pl.when(p <= 1)
    def _():
        rm[...] = jnp.zeros_like(rm)

    @pl.when(p == 3)
    def _():
        b1[...] = jnp.zeros_like(b1)

    @pl.when(p >= 2)
    def _():
        b2[...] = jnp.zeros_like(b2)

    @pl.when(p >= 1)
    def _():
        b3[...] = jnp.zeros_like(b3)


    def local_state(h, _):
        kept = take(0, h) * keep[...].astype(BF16)
        own[h] = mm(kept, take(1, h), 0, 0)
        own_c[h] = encode(own[h])
        return 0


    def move(src, dst, c, send, recv, to):
        return pltpu.make_async_remote_copy(
            src_ref=src.at[c], dst_ref=dst.at[c], send_sem=send.at[c], recv_sem=recv.at[c],
            device_id=(to, t, y), device_id_type=MESH,
        )

    def plus(src, c):
        return move(src, rp, c, plus_send, rp_recv, after)

    def minus(src, c):
        return move(src, rm, c, minus_send, rm_recv, before)

    def back1(c):
        return move(sg_c, b1, c, b1_send, b1_recv, before)

    def back2(c):
        return move(sg_c, b2, c, b2_send, b2_recv, lax.rem(z + SEQ - 2 * GZ, SEQ))

    def back3(c):
        return move(sg_c, b3, c, b3_send, b3_recv, after)

    def forward(c, _):
        @pl.when(p <= 1)
        def _():
            plus(own_c, c).start()

        @pl.when(p == 0)
        def _():
            minus(own_c, c).start()

        @pl.when(p == 2)
        def _():
            plus(own_c, c).wait_recv()
            fsend[c] = encode(own[c] + carry * decode(rp[c]))
            plus(fsend, c).start()

        @pl.when(p == 3)
        def _():
            minus(rm, c).wait_recv()
            minus(rm, c).start()

        return 0

    def forward_rest(c, _):
        @pl.when((p == 1) | (p == 3))
        def _():
            plus(own_c, c).wait_recv()

        @pl.when(p == 2)
        def _():
            minus(rm, c).wait_recv()

        return 0

    def local_scores(h, _):
        for r in range(2):
            n = HALF * (r + 1)
            at = pl.ds(r * HALF, HALF)
            scores[h, at, pl.ds(0, n)] = (
                mm(take(2, h, r * HALF, HALF), take(0, h, 0, n), 1, 1) * mask[at, pl.ds(0, n)]
            )
            sh, sl = split(scores[h, at, pl.ds(0, n)])
            value = take(1, h, 0, n)
            inner[h, at, :] = mm(sh, value) + mm(sl, value)
        return 0

    def attend(h, _):
        pltpu.make_async_copy(qc.at[h], qc.at[h], qc_recv.at[h]).wait()
        local_scores(h, 0)
        forward_rest(h, 0)
        state = decode(rp[h]) + far_in * decode(rm[h])
        states[h] = state
        th, tl = split(state)
        at = j * HEADS + h
        gain = gain_ref[pl.ds(at, 1), :]
        gain_part = jnp.zeros((1, DIM), F32)
        state_grad = jnp.zeros((DIM, DIM), F32)
        for r in range(2):
            n = HALF * (r + 1)
            rr = pl.ds(r * HALF, HALF)
            query = take(2, h, r * HALF, HALF)
            used = use[rr, :]
            att = inner[h, rr, :] + used * (mm(query, th) + mm(query, tl))
            centered = att - jnp.mean(att, axis=-1, keepdims=True)
            inv = lax.rsqrt(jnp.mean(centered * centered, axis=-1, keepdims=True) + EPSILON)
            normed = centered * inv
            up = take(3, h, r * HALF, HALF).astype(F32)
            gain_part = gain_part + jnp.sum(up * normed, axis=0, keepdims=True)
            dn = up * gain
            d_att = inv * (
                dn
                - jnp.mean(dn, axis=-1, keepdims=True)
                - normed * jnp.mean(dn * normed, axis=-1, keepdims=True)
            )
            hi, lo = split(d_att)
            dh[h, rr, :] = hi
            dl[h, rr, :] = lo
            used = used.astype(BF16)
            state_grad = state_grad + mm(query, hi * used, 0, 0) + mm(query, lo * used, 0, 0)
        gsrc[pl.ds(at, 1), :] = gain_part
        sg_c[h] = encode(state_grad)

        @pl.when(p == 3)
        def _():
            back3(h).start()

        @pl.when(p >= 2)
        def _():
            back2(h).start()

        @pl.when(p >= 1)
        def _():
            back1(h).start()

        return 0

    def states_of(h, _):
        pltpu.make_async_copy(kv.at[h], kv.at[h], kv_recv.at[h]).wait()
        local_state(h, 0)

        @pl.when((h == 0) & (p < POS - 1))
        def _():
            pl.semaphore_wait(ready.at[0], 1)

        @pl.when((h == 0) & (p == 0))
        def _():
            pl.semaphore_wait(ready.at[1], 1)

        forward(h, 0)

        @pl.when(p <= 1)
        def _():
            send_qc(h)

        @pl.when(h == 0)
        def _():
            send_kv(1)

        @pl.when((h == 0) & (p >= 2))
        def _():
            send_qc(1)

        attend(h, 0)
        return 0

    lax.fori_loop(0, HEADS, states_of, 0)

    gy[y] = gsrc[...]

    def gy_copy(yy):
        return pltpu.make_async_remote_copy(
            src_ref=gy.at[y], dst_ref=gy.at[y], send_sem=gy_send.at[yy], recv_sem=gy_recv.at[y],
            device_id=(z, t, yy), device_id_type=MESH,
        )

    for yy in range(1, 4):
        @pl.when(yy > y)
        def _():
            pl.semaphore_wait(ready_y.at[yy], 1)

    for s in range(1, 4):
        gy_copy(lax.rem(y + s, 4)).start()

    def backward(c, _):
        @pl.when(p <= 2)
        def _():
            back1(c).wait_recv()

        @pl.when(p <= 1)
        def _():
            back2(c).wait_recv()

        @pl.when(p == 0)
        def _():
            back3(c).wait_recv()

        return 0

    def send_dq(h):
        cols = pl.ds(pl.multiple_of(t * 1024 + j * COLS + h * DIM, DIM), DIM)

        def body(s, _):
            g, jj, tt = peer(s)
            at = pl.ds(pl.multiple_of(g * ROWS, ROWS), ROWS)
            to_heads(dq.at[h, at, :], out_ref.at[0, :, cols], jj, tt, dq_send.at[h], dq_recv.at[h]).start()
            return 0

        lax.fori_loop(1, GROUP, body, 0)
        pltpu.make_async_copy(dq.at[h, mine, :], out_ref.at[0, :, cols], dq_recv.at[h]).start()

    def send_dkv(h):
        cols = pl.ds(pl.multiple_of(t * 1024 + j * COLS + h * DIM, DIM), DIM)

        def body(s, _):
            g, jj, tt = peer(s)
            at = pl.ds(pl.multiple_of(g * ROWS, ROWS), ROWS)
            to_heads(
                dkv.at[h, :, at, :], out_ref.at[pl.ds(1, 2), :, cols], jj, tt, dkv_send.at[h], dkv_recv.at[h]
            ).start()
            return 0

        lax.fori_loop(1, GROUP, body, 0)
        pltpu.make_async_copy(dkv.at[h, :, mine, :], out_ref.at[pl.ds(1, 2), :, cols], dkv_recv.at[h]).start()

    def local_grads(h, _):
        th, tl = split(states[h])
        for r in range(2):
            n = HALF * (r + 1)
            rr, cc = pl.ds(r * HALF, HALF), pl.ds(0, n)
            key, value, query = take(0, h, 0, n), take(1, h, 0, n), take(2, h, r * HALF, HALF)
            hi, lo = dh[h, rr, :], dl[h, rr, :]
            d_sc = (mm(hi, value, 1, 1) + mm(lo, value, 1, 1)) * mask[rr, cc]
            eh, el = split(d_sc)
            sh, sl = split(scores[h, rr, cc])
            d_query = mm(eh, key) + mm(el, key)
            d_query = d_query + use[rr, :] * (mm(hi, th, 1, 1) + mm(hi, tl, 1, 1) + mm(lo, th, 1, 1))
            dq[h, rr, :] = d_query.astype(BF16)
            d_key = mm(eh, query, 0, 0) + mm(el, query, 0, 0)
            d_value = mm(sh, hi, 0, 0) + mm(sl, hi, 0, 0) + mm(sh, lo, 0, 0)
            if r == 0:
                dkl[h, rr, :] = d_key
                dvl[h, rr, :] = d_value
            else:
                low = pl.ds(0, HALF)
                dkl[h, low, :] += d_key[:HALF]
                dvl[h, low, :] += d_value[:HALF]
                dkl[h, rr, :] = d_key[HALF:]
                dvl[h, rr, :] = d_value[HALF:]
        return 0

    def gg_copy(s):
        return pltpu.make_async_remote_copy(
            src_ref=gg.at[j], dst_ref=gg.at[j], send_sem=gg_send.at[s], recv_sem=gg_recv.at[j],
            device_id=(base + lax.rem(j + s, GZ), t, y), device_id_type=MESH,
        )

    even = lax.rem(p, 2) == 0
    near = jnp.where(even, after, before)
    other = jnp.where(even, before, after)

    def gz_copy(i, partner):
        return pltpu.make_async_remote_copy(
            src_ref=gz.at[2 * i], dst_ref=gz.at[2 * i + 1], send_sem=gz_send.at[i], recv_sem=gz_recv.at[i],
            device_id=(partner, t, y), device_id_type=MESH,
        )

    def last_grads(h, _):
        local_grads(h, 0)
        send_dq(h)

        @pl.when(h == 0)
        def _():
            for s in range(1, 4):
                yy = lax.rem(y + s, 4)
                pltpu.make_async_copy(gy.at[yy], gy.at[yy], gy_recv.at[yy]).wait()
            gg[j] = (gy[0] + gy[1]) + (gy[2] + gy[3])
            for s in range(1, GZ):
                gg_copy(s).start()

        backward(h, 0)
        gh, gl = split(decode(b1[h]) + out2 * decode(b2[h]) + out3 * decode(b3[h]))
        key, value = take(0, h), take(1, h)
        d_key = dkl[h] + keep[...] * (mm(value, gh, 1, 1) + mm(value, gl, 1, 1))
        d_value = dvl[h] + keep[...] * (mm(key, gh) + mm(key, gl))
        dkv[h, 0] = d_key.astype(BF16)
        dkv[h, 1] = d_value.astype(BF16)
        send_dkv(h)

        @pl.when(h == 0)
        def _():
            for s in range(1, GZ):
                jj = lax.rem(j + s, GZ)
                pltpu.make_async_copy(gg.at[jj], gg.at[jj], gg_recv.at[jj]).wait()
            gz[0] = (gg[0] + gg[1]) + (gg[2] + gg[3])
            gz_copy(0, near).start()

        return 0

    lax.fori_loop(0, HEADS, last_grads, 0)
    gz_copy(0, near).wait_recv()
    gz[2] = gz[0] + gz[1]
    gz_copy(1, other).start()
    gz_copy(1, other).wait_recv()
    gout_ref[...] = (gz[2] + gz[3]) / math.sqrt(4 * SEQ * 128)

    half = pl.ds(0, 4096)
    for h in range(HEADS):
        part = out_ref.at[0, :, half]
        pltpu.make_async_copy(part, part, dq_recv.at[h]).wait()
        pltpu.make_async_copy(out_ref.at[1 + h], out_ref.at[1 + h], dkv_recv.at[h]).wait()
    most = pl.ds(0, TOK - ROWS)
    for h in range(HEADS):
        for ref, sem in ((kv, kv_send), (qc, qc_send), (dkv, dkv_send)):
            part = ref.at[h, :, most, :]
            pltpu.make_async_copy(part, part, sem.at[h]).wait()
        part = dq.at[h, most, :]
        pltpu.make_async_copy(part, part, dq_send.at[h]).wait()
    gz_copy(0, near).wait_send()
    gz_copy(1, other).wait_send()
    for s in range(1, GZ):
        gg_copy(s).wait_send()
    for s in range(1, 4):
        gy_copy(lax.rem(y + s, 4)).wait_send()

    def drain(c, _):
        @pl.when(p <= 2)
        def _():
            plus(own_c, c).wait_send()

        @pl.when((p == 0) | (p == 3))
        def _():
            minus(own_c, c).wait_send()

        @pl.when(p == 3)
        def _():
            back3(c).wait_send()

        @pl.when(p >= 2)
        def _():
            back2(c).wait_send()

        @pl.when(p >= 1)
        def _():
            back1(c).wait_send()

        return 0

    lax.fori_loop(0, HEADS, drain, 0)


def place(grads_ref, gain_ref, q_ref, k_ref, v_ref, g_ref, sems):
    copies = [
        pltpu.make_async_copy(grads_ref.at[i], ref.at[0], sems.at[i])
        for i, ref in enumerate((q_ref, k_ref, v_ref))
    ]
    for copy in copies:
        copy.start()
    g_ref[...] = gain_ref[...]
    for copy in copies:
        copy.wait()


def local(query_rows, key_rows, value_rows, cotangent, norm_gain, doc_starts):
    anywhere = pl.BlockSpec(memory_space=pl.ANY)
    hbm = pl.BlockSpec(memory_space=pltpu.HBM)
    vmem = pl.BlockSpec(memory_space=pltpu.VMEM)
    smem = pl.BlockSpec(memory_space=pltpu.SMEM)
    dma = pltpu.SemaphoreType.DMA
    state = pltpu.VMEM((HEADS, DIM, DIM), F32)
    coded = pltpu.VMEM((HEADS, CODED, DIM), jnp.int16)
    grads, gain_sum = pl.pallas_call(
        kernel,
        out_shape=(
            jax.ShapeDtypeStruct((3, ROWS, 8192), BF16),
            jax.ShapeDtypeStruct((8, DIM), F32),
        ),
        in_specs=[hbm] * 6,
        out_specs=(anywhere, vmem),
        scratch_shapes=[
            pltpu.VMEM((4, ROWS, 8192), BF16),
            pltpu.VMEM((HEADS, 2, TOK, DIM), BF16),
            pltpu.VMEM((HEADS, 2, TOK, DIM), BF16),
            pltpu.VMEM((TOK, TOK), F32),
            pltpu.VMEM((TOK, DIM), F32),
            pltpu.VMEM((TOK, DIM), F32),
            state, coded, coded, coded, coded, state, coded, coded, coded, coded,
            pltpu.VMEM((HEADS, TOK, DIM), F32),
            pltpu.VMEM((HEADS, TOK, TOK), F32),
            pltpu.VMEM((HEADS, TOK, DIM), BF16),
            pltpu.VMEM((HEADS, TOK, DIM), BF16),
            pltpu.VMEM((HEADS, TOK, DIM), F32),
            pltpu.VMEM((HEADS, TOK, DIM), F32),
            pltpu.VMEM((HEADS, TOK, DIM), BF16),
            pltpu.VMEM((HEADS, 2, TOK, DIM), BF16),
            pltpu.VMEM((8, DIM), F32),
            pltpu.VMEM((4, 8, DIM), F32),
            pltpu.VMEM((GZ, 8, DIM), F32),
            pltpu.VMEM((4, 8, DIM), F32),
            dma((4,)), dma((HEADS,)), dma((HEADS,)), dma((HEADS,)), dma((HEADS,)),
            dma((HEADS,)), dma((HEADS,)), dma((HEADS,)), dma((HEADS,)), dma((HEADS,)),
            dma((HEADS,)), dma((HEADS,)), dma((HEADS,)), dma((HEADS,)), dma((HEADS,)),
            dma((HEADS,)), dma((HEADS,)), dma((HEADS,)), dma((HEADS,)),
            dma((4,)), dma((4,)), dma((GZ,)), dma((GZ,)), dma((2,)), dma((2,)),
            pltpu.SemaphoreType.REGULAR((2,)), pltpu.SemaphoreType.REGULAR((4,)),
            pltpu.VMEM((8, DIM), F32), pltpu.SMEM((1, 8), jnp.int32), dma((2,)),
        ],
        compiler_params=pltpu.CompilerParams(
            collective_id=1, has_side_effects=True, vmem_limit_bytes=60 * 1024 * 1024
        ),
        name="layer",
    )(key_rows, value_rows, query_rows, cotangent, norm_gain.reshape(8, DIM), doc_starts)
    rows = jax.ShapeDtypeStruct((1, ROWS, 8192), BF16)
    grad_q, grad_k, grad_v, gain = pl.pallas_call(
        place,
        out_shape=(rows, rows, rows, jax.ShapeDtypeStruct((8, DIM), F32)),
        in_specs=[vmem, vmem],
        out_specs=(anywhere, anywhere, anywhere, vmem),
        scratch_shapes=[dma((3,))],
        name="place",
    )(grads, gain_sum)
    return grad_q, grad_k, grad_v, gain.reshape(8 * DIM)


def solution(mesh):
    rows = P("dp", ("seq", "tensor"), None)
    return jax.shard_map(
        local,
        mesh=mesh,
        in_specs=(rows, rows, rows, rows, P("tensor"), P("dp", None)),
        out_specs=(rows, rows, rows, P("tensor")),
        check_vma=False,
    )
```

```python
import functools
import math

import jax
import jax.numpy as jnp
from jax import lax
from jax.experimental import pallas as pl
from jax.experimental.pallas import tpu as pltpu
from jax.sharding import PartitionSpec as P

MESH = pl.DeviceIdType.MESH
F32 = jnp.float32
BF16 = jnp.bfloat16
EPSILON = 1e-05
DIM = 128
HEADS = 2
GZ = 4
POS = 4
TOK = 512
HALF = 256
COLS = HEADS * DIM
ROWS = 16
GROUP = 32
SEQ = 16
CODED = DIM + 16


def split(x):
    hi = x.astype(BF16)
    return hi, (x - hi.astype(F32)).astype(BF16)


def encode(x):
    top = jnp.maximum(jnp.max(jnp.abs(x), axis=0, keepdims=True), 1e-30)
    power = jnp.floor(jnp.log(top) * (1 / math.log(2)))
    coded = jnp.clip(jnp.floor(x * jnp.exp2(14 - power) + 0.5), -32767, 32767)
    rows = jnp.concatenate([coded, jnp.broadcast_to(power, (CODED - DIM, DIM))], axis=0)
    return rows.astype(jnp.int32).astype(jnp.int16)


def decode(coded):
    values = coded.astype(jnp.int32).astype(F32)
    return values[:DIM] * jnp.exp2(values[DIM : DIM + 1] - 14)


def mm(a, b, ca=1, cb=0):
    return lax.dot_general(a, b, (((ca,), (cb,)), ((), ())), preferred_element_type=F32)


def kernel(
    k_ref, v_ref, q_ref, c_ref, gain_in, starts_in,
    out_ref, gout_ref,
    stage, kv, qc, mask, use, keep, own, own_c, fsend, rp, rm, states, sg_c, b1, b2, b3, inner, scores, dh, dl, dkl, dvl, dq, dkv,
    gsrc, gy, gg, gz,
    st_sem, kv_send, kv_recv, qc_send, qc_recv,
    plus_send, rp_recv, minus_send, rm_recv, b1_send, b1_recv, b2_send, b2_recv, b3_send, b3_recv,
    dq_send, dq_recv, dkv_send, dkv_recv, gy_send, gy_recv, gg_send, gg_recv, gz_send, gz_recv, ready, ready_y, gain_ref, starts_ref, small_sem,
):
    z, t, y = lax.axis_index("seq"), lax.axis_index("tensor"), lax.axis_index("dp")
    p, j = z // GZ, lax.rem(z, GZ)
    base = p * GZ
    me = j * 8 + t
    after, before = lax.rem(z + GZ, SEQ), lax.rem(z + SEQ - GZ, SEQ)

    def peer(s):
        g = lax.rem(me + s, GROUP)
        return g, g // 8, lax.rem(g, 8)

    def staged(a, ref):
        return pltpu.make_async_copy(ref.at[0], stage.at[a], st_sem.at[a])

    rows_in = ((0, k_ref), (1, v_ref), (2, q_ref), (3, c_ref))
    for a, ref in rows_in:
        staged(a, ref).start()

    small = (
        pltpu.make_async_copy(gain_in, gain_ref, small_sem.at[0]),
        pltpu.make_async_copy(starts_in, starts_ref, small_sem.at[1]),
    )
    for copy in small:
        copy.start()

    barrier = pltpu.get_barrier_semaphore()

    def greet(zz, tt, yy):
        pl.semaphore_signal(barrier, inc=1, device_id=(zz, tt, yy), device_id_type=MESH)

    for d in range(1, POS):
        @pl.when(p + d < POS)
        def _():
            greet(lax.rem(z + d * GZ, SEQ), t, y)

    for yy in range(1, 4):
        @pl.when(yy > y)
        def _():
            greet(z, t, yy)

    def greet_group(s, _):
        _, jj, tt = peer(s)
        greet(base + jj, tt, y)
        return 0

    lax.fori_loop(1, GROUP, greet_group, 0)

    pl.semaphore_wait(barrier, 31 + y + p)

    def answer(sem, zz, yy):
        pl.semaphore_signal(sem, inc=1, device_id=(zz, t, yy), device_id_type=MESH)

    for d in range(1, POS):
        @pl.when(p - d >= 0)
        def _():
            answer(ready.at[d - 1], lax.rem(z + SEQ - d * GZ, SEQ), y)

    for yy in range(3):
        @pl.when(yy < y)
        def _():
            answer(ready_y.at[y], z, yy)

    mine = pl.ds(pl.multiple_of(me * ROWS, ROWS), ROWS)
    my_cols = pl.ds(pl.multiple_of(t * 1024 + j * COLS, COLS), COLS)

    def to_heads(src, dst, jj, tt, send, recv):
        return pltpu.make_async_remote_copy(
            src_ref=src, dst_ref=dst, send_sem=send, recv_sem=recv,
            device_id=(base + jj, tt, y), device_id_type=MESH,
        )

    def send_in(first_row, dst, send, recv, h):
        def part(tt, jj):
            cols = pl.ds(pl.multiple_of(tt * 1024 + jj * COLS + h * DIM, DIM), DIM)
            return stage.at[pl.ds(first_row, 2), :, cols]

        def body(s, _):
            g, jj, tt = peer(s)
            to_heads(part(tt, jj), dst.at[h, :, mine, :], jj, tt, send.at[h], recv.at[h]).start()
            return 0

        lax.fori_loop(1, GROUP, body, 0)
        pltpu.make_async_copy(part(t, j), dst.at[h, :, mine, :], recv.at[h]).start()

    def send_kv(h):
        send_in(0, kv, kv_send, kv_recv, h)

    def send_qc(h):
        send_in(2, qc, qc_send, qc_recv, h)

    staged(0, k_ref).wait()
    staged(1, v_ref).wait()
    send_kv(0)
    staged(2, q_ref).wait()
    staged(3, c_ref).wait()

    @pl.when(p >= 2)
    def _():
        send_qc(0)

    def take(a, h, start=0, size=TOK):
        if a < 2:
            return kv[h, a, pl.ds(start, size), :]
        return qc[h, a - 2, pl.ds(start, size), :]

    def count(tok):
        total = jnp.zeros_like(tok)
        for i in range(8):
            total = total + (starts_ref[0, i] <= tok).astype(jnp.int32)
        return total

    for copy in small:
        copy.wait()
    first = base * 128
    prev = count(first - 1)
    last = count(first + TOK - 1)
    carry = (prev == last).astype(F32)
    far_in = (count(TOK - 1) == prev).astype(F32)
    out2 = (last == count(first + 2 * TOK - 1)).astype(F32)
    out3 = (last == count(first + 3 * TOK - 1)).astype(F32)
    row = lax.broadcasted_iota(jnp.int32, (TOK, DIM), 0) + first
    seg = count(row)
    use[...] = (seg == prev).astype(F32)
    keep[...] = (seg == last).astype(F32)
    seg_row = count(lax.broadcasted_iota(jnp.int32, (8, TOK), 1) + first)[:1]
    seg_col = jnp.concatenate([seg] * 4, axis=1)
    rows = lax.broadcasted_iota(jnp.int32, (TOK, TOK), 0)
    cols = lax.broadcasted_iota(jnp.int32, (TOK, TOK), 1)
    mask[...] = ((rows >= cols) & (seg_col == seg_row)).astype(F32)
    gsrc[...] = jnp.zeros_like(gsrc)

    @pl.when(p == 0)
    def _():
        rp[...] = jnp.zeros_like(rp)

    @pl.when(p <= 1)
    def _():
        rm[...] = jnp.zeros_like(rm)

    @pl.when(p == 3)
    def _():
        b1[...] = jnp.zeros_like(b1)

    @pl.when(p >= 2)
    def _():
        b2[...] = jnp.zeros_like(b2)

    @pl.when(p >= 1)
    def _():
        b3[...] = jnp.zeros_like(b3)


    def local_state(h, _):
        kept = take(0, h) * keep[...].astype(BF16)
        own[h] = mm(kept, take(1, h), 0, 0)
        own_c[h] = encode(own[h])
        return 0


    def move(src, dst, c, send, recv, to):
        return pltpu.make_async_remote_copy(
            src_ref=src.at[c], dst_ref=dst.at[c], send_sem=send.at[c], recv_sem=recv.at[c],
            device_id=(to, t, y), device_id_type=MESH,
        )

    def plus(src, c):
        return move(src, rp, c, plus_send, rp_recv, after)

    def minus(src, c):
        return move(src, rm, c, minus_send, rm_recv, before)

    def back1(c):
        return move(sg_c, b1, c, b1_send, b1_recv, before)

    def back2(c):
        return move(sg_c, b2, c, b2_send, b2_recv, lax.rem(z + SEQ - 2 * GZ, SEQ))

    def back3(c):
        return move(sg_c, b3, c, b3_send, b3_recv, after)

    def forward(c, _):
        @pl.when(p <= 1)
        def _():
            plus(own_c, c).start()

        @pl.when(p == 0)
        def _():
            minus(own_c, c).start()

        @pl.when(p == 2)
        def _():
            plus(own_c, c).wait_recv()
            fsend[c] = encode(own[c] + carry * decode(rp[c]))
            plus(fsend, c).start()

        @pl.when(p == 3)
        def _():
            minus(rm, c).wait_recv()
            minus(rm, c).start()

        return 0

    def forward_rest(c, _):
        @pl.when((p == 1) | (p == 3))
        def _():
            plus(own_c, c).wait_recv()

        @pl.when(p == 2)
        def _():
            minus(rm, c).wait_recv()

        return 0

    def local_scores(h, _):
        for r in range(2):
            n = HALF * (r + 1)
            at = pl.ds(r * HALF, HALF)
            scores[h, at, pl.ds(0, n)] = (
                mm(take(2, h, r * HALF, HALF), take(0, h, 0, n), 1, 1) * mask[at, pl.ds(0, n)]
            )
            sh, sl = split(scores[h, at, pl.ds(0, n)])
            value = take(1, h, 0, n)
            inner[h, at, :] = mm(sh, value) + mm(sl, value)
        return 0

    def attend(h, _):
        pltpu.make_async_copy(qc.at[h], qc.at[h], qc_recv.at[h]).wait()
        local_scores(h, 0)
        forward_rest(h, 0)
        state = decode(rp[h]) + far_in * decode(rm[h])
        states[h] = state
        th, tl = split(state)
        at = j * HEADS + h
        gain = gain_ref[pl.ds(at, 1), :]
        gain_part = jnp.zeros((1, DIM), F32)
        state_grad = jnp.zeros((DIM, DIM), F32)
        for r in range(2):
            n = HALF * (r + 1)
            rr = pl.ds(r * HALF, HALF)
            query = take(2, h, r * HALF, HALF)
            used = use[rr, :]
            att = inner[h, rr, :] + used * (mm(query, th) + mm(query, tl))
            centered = att - jnp.mean(att, axis=-1, keepdims=True)
            inv = lax.rsqrt(jnp.mean(centered * centered, axis=-1, keepdims=True) + EPSILON)
            normed = centered * inv
            up = take(3, h, r * HALF, HALF).astype(F32)
            gain_part = gain_part + jnp.sum(up * normed, axis=0, keepdims=True)
            dn = up * gain
            d_att = inv * (
                dn
                - jnp.mean(dn, axis=-1, keepdims=True)
                - normed * jnp.mean(dn * normed, axis=-1, keepdims=True)
            )
            hi, lo = split(d_att)
            dh[h, rr, :] = hi
            dl[h, rr, :] = lo
            used = used.astype(BF16)
            state_grad = state_grad + mm(query, hi * used, 0, 0) + mm(query, lo * used, 0, 0)
        gsrc[pl.ds(at, 1), :] = gain_part
        sg_c[h] = encode(state_grad)

        @pl.when(p == 3)
        def _():
            back3(h).start()

        @pl.when(p >= 2)
        def _():
            back2(h).start()

        @pl.when(p >= 1)
        def _():
            back1(h).start()

        return 0

    def states_of(h, _):
        pltpu.make_async_copy(kv.at[h], kv.at[h], kv_recv.at[h]).wait()
        local_state(h, 0)

        @pl.when((h == 0) & (p < POS - 1))
        def _():
            pl.semaphore_wait(ready.at[0], 1)

        @pl.when((h == 0) & (p == 0))
        def _():
            pl.semaphore_wait(ready.at[2], 1)

        forward(h, 0)

        @pl.when(p <= 1)
        def _():
            send_qc(h)

        @pl.when(h == 0)
        def _():
            send_kv(1)

        @pl.when((h == 0) & (p >= 2))
        def _():
            send_qc(1)

        attend(h, 0)
        return 0

    lax.fori_loop(0, HEADS, states_of, 0)

    gy[y] = gsrc[...]

    def gy_copy(yy):
        return pltpu.make_async_remote_copy(
            src_ref=gy.at[y], dst_ref=gy.at[y], send_sem=gy_send.at[yy], recv_sem=gy_recv.at[y],
            device_id=(z, t, yy), device_id_type=MESH,
        )

    for yy in range(1, 4):
        @pl.when(yy > y)
        def _():
            pl.semaphore_wait(ready_y.at[yy], 1)

    for s in range(1, 4):
        gy_copy(lax.rem(y + s, 4)).start()

    def backward(c, _):
        @pl.when(p <= 2)
        def _():
            back1(c).wait_recv()

        @pl.when(p <= 1)
        def _():
            back2(c).wait_recv()

        @pl.when(p == 0)
        def _():
            back3(c).wait_recv()

        return 0

    def send_dq(h):
        cols = pl.ds(pl.multiple_of(t * 1024 + j * COLS + h * DIM, DIM), DIM)

        def body(s, _):
            g, jj, tt = peer(s)
            at = pl.ds(pl.multiple_of(g * ROWS, ROWS), ROWS)
            to_heads(dq.at[h, at, :], out_ref.at[0, :, cols], jj, tt, dq_send.at[h], dq_recv.at[h]).start()
            return 0

        lax.fori_loop(1, GROUP, body, 0)
        pltpu.make_async_copy(dq.at[h, mine, :], out_ref.at[0, :, cols], dq_recv.at[h]).start()

    def send_dkv(h):
        cols = pl.ds(pl.multiple_of(t * 1024 + j * COLS + h * DIM, DIM), DIM)

        def body(s, _):
            g, jj, tt = peer(s)
            at = pl.ds(pl.multiple_of(g * ROWS, ROWS), ROWS)
            to_heads(
                dkv.at[h, :, at, :], out_ref.at[pl.ds(1, 2), :, cols], jj, tt, dkv_send.at[h], dkv_recv.at[h]
            ).start()
            return 0

        lax.fori_loop(1, GROUP, body, 0)
        pltpu.make_async_copy(dkv.at[h, :, mine, :], out_ref.at[pl.ds(1, 2), :, cols], dkv_recv.at[h]).start()

    def local_grads(h, _):
        th, tl = split(states[h])
        for r in range(2):
            n = HALF * (r + 1)
            rr, cc = pl.ds(r * HALF, HALF), pl.ds(0, n)
            key, value, query = take(0, h, 0, n), take(1, h, 0, n), take(2, h, r * HALF, HALF)
            hi, lo = dh[h, rr, :], dl[h, rr, :]
            d_sc = (mm(hi, value, 1, 1) + mm(lo, value, 1, 1)) * mask[rr, cc]
            eh, el = split(d_sc)
            sh, sl = split(scores[h, rr, cc])
            d_query = mm(eh, key) + mm(el, key)
            d_query = d_query + use[rr, :] * (mm(hi, th, 1, 1) + mm(hi, tl, 1, 1) + mm(lo, th, 1, 1))
            dq[h, rr, :] = d_query.astype(BF16)
            d_key = mm(eh, query, 0, 0) + mm(el, query, 0, 0)
            d_value = mm(sh, hi, 0, 0) + mm(sl, hi, 0, 0) + mm(sh, lo, 0, 0)
            if r == 0:
                dkl[h, rr, :] = d_key
                dvl[h, rr, :] = d_value
            else:
                low = pl.ds(0, HALF)
                dkl[h, low, :] += d_key[:HALF]
                dvl[h, low, :] += d_value[:HALF]
                dkl[h, rr, :] = d_key[HALF:]
                dvl[h, rr, :] = d_value[HALF:]
        return 0

    def gg_copy(s):
        return pltpu.make_async_remote_copy(
            src_ref=gg.at[j], dst_ref=gg.at[j], send_sem=gg_send.at[s], recv_sem=gg_recv.at[j],
            device_id=(base + lax.rem(j + s, GZ), t, y), device_id_type=MESH,
        )

    def gz_copy(d):
        return pltpu.make_async_remote_copy(
            src_ref=gz.at[p], dst_ref=gz.at[p], send_sem=gz_send.at[d - 1], recv_sem=gz_recv.at[d - 1],
            device_id=(lax.rem(z + d * GZ, SEQ), t, y), device_id_type=MESH,
        )

    def last_grads(h, _):
        local_grads(h, 0)
        send_dq(h)

        @pl.when(h == 0)
        def _():
            for s in range(1, 4):
                yy = lax.rem(y + s, 4)
                pltpu.make_async_copy(gy.at[yy], gy.at[yy], gy_recv.at[yy]).wait()
            gg[j] = (gy[0] + gy[1]) + (gy[2] + gy[3])
            for s in range(1, GZ):
                gg_copy(s).start()

        backward(h, 0)
        gh, gl = split(decode(b1[h]) + out2 * decode(b2[h]) + out3 * decode(b3[h]))
        key, value = take(0, h), take(1, h)
        d_key = dkl[h] + keep[...] * (mm(value, gh, 1, 1) + mm(value, gl, 1, 1))
        d_value = dvl[h] + keep[...] * (mm(key, gh) + mm(key, gl))
        dkv[h, 0] = d_key.astype(BF16)
        dkv[h, 1] = d_value.astype(BF16)
        send_dkv(h)

        @pl.when(h == 0)
        def _():
            for s in range(1, GZ):
                jj = lax.rem(j + s, GZ)
                pltpu.make_async_copy(gg.at[jj], gg.at[jj], gg_recv.at[jj]).wait()
            gz[p] = (gg[0] + gg[1]) + (gg[2] + gg[3])

            @pl.when(p <= 1)
            def _():
                pl.semaphore_wait(ready.at[1], 1)

            for d in range(1, POS):
                gz_copy(d).start()

        return 0

    lax.fori_loop(0, HEADS, last_grads, 0)
    for d in range(1, POS):
        gz_copy(d).wait_recv()
    gout_ref[...] = ((gz[0] + gz[1]) + (gz[2] + gz[3])) / math.sqrt(4 * SEQ * 128)

    half = pl.ds(0, 4096)
    for h in range(HEADS):
        part = out_ref.at[0, :, half]
        pltpu.make_async_copy(part, part, dq_recv.at[h]).wait()
        pltpu.make_async_copy(out_ref.at[1 + h], out_ref.at[1 + h], dkv_recv.at[h]).wait()
    most = pl.ds(0, TOK - ROWS)
    for h in range(HEADS):
        for ref, sem in ((kv, kv_send), (qc, qc_send), (dkv, dkv_send)):
            part = ref.at[h, :, most, :]
            pltpu.make_async_copy(part, part, sem.at[h]).wait()
        part = dq.at[h, most, :]
        pltpu.make_async_copy(part, part, dq_send.at[h]).wait()
    for d in range(1, POS):
        gz_copy(d).wait_send()
    for s in range(1, GZ):
        gg_copy(s).wait_send()
    for s in range(1, 4):
        gy_copy(lax.rem(y + s, 4)).wait_send()

    def drain(c, _):
        @pl.when(p <= 2)
        def _():
            plus(own_c, c).wait_send()

        @pl.when((p == 0) | (p == 3))
        def _():
            minus(own_c, c).wait_send()

        @pl.when(p == 3)
        def _():
            back3(c).wait_send()

        @pl.when(p >= 2)
        def _():
            back2(c).wait_send()

        @pl.when(p >= 1)
        def _():
            back1(c).wait_send()

        return 0

    lax.fori_loop(0, HEADS, drain, 0)


def place(grads_ref, gain_ref, q_ref, k_ref, v_ref, g_ref, sems):
    copies = [
        pltpu.make_async_copy(grads_ref.at[i], ref.at[0], sems.at[i])
        for i, ref in enumerate((q_ref, k_ref, v_ref))
    ]
    for copy in copies:
        copy.start()
    g_ref[...] = gain_ref[...]
    for copy in copies:
        copy.wait()


def local(query_rows, key_rows, value_rows, cotangent, norm_gain, doc_starts):
    anywhere = pl.BlockSpec(memory_space=pl.ANY)
    hbm = pl.BlockSpec(memory_space=pltpu.HBM)
    vmem = pl.BlockSpec(memory_space=pltpu.VMEM)
    smem = pl.BlockSpec(memory_space=pltpu.SMEM)
    dma = pltpu.SemaphoreType.DMA
    state = pltpu.VMEM((HEADS, DIM, DIM), F32)
    coded = pltpu.VMEM((HEADS, CODED, DIM), jnp.int16)
    grads, gain_sum = pl.pallas_call(
        kernel,
        out_shape=(
            jax.ShapeDtypeStruct((3, ROWS, 8192), BF16),
            jax.ShapeDtypeStruct((8, DIM), F32),
        ),
        in_specs=[hbm] * 6,
        out_specs=(anywhere, vmem),
        scratch_shapes=[
            pltpu.VMEM((4, ROWS, 8192), BF16),
            pltpu.VMEM((HEADS, 2, TOK, DIM), BF16),
            pltpu.VMEM((HEADS, 2, TOK, DIM), BF16),
            pltpu.VMEM((TOK, TOK), F32),
            pltpu.VMEM((TOK, DIM), F32),
            pltpu.VMEM((TOK, DIM), F32),
            state, coded, coded, coded, coded, state, coded, coded, coded, coded,
            pltpu.VMEM((HEADS, TOK, DIM), F32),
            pltpu.VMEM((HEADS, TOK, TOK), F32),
            pltpu.VMEM((HEADS, TOK, DIM), BF16),
            pltpu.VMEM((HEADS, TOK, DIM), BF16),
            pltpu.VMEM((HEADS, TOK, DIM), F32),
            pltpu.VMEM((HEADS, TOK, DIM), F32),
            pltpu.VMEM((HEADS, TOK, DIM), BF16),
            pltpu.VMEM((HEADS, 2, TOK, DIM), BF16),
            pltpu.VMEM((8, DIM), F32),
            pltpu.VMEM((4, 8, DIM), F32),
            pltpu.VMEM((GZ, 8, DIM), F32),
            pltpu.VMEM((4, 8, DIM), F32),
            dma((4,)), dma((HEADS,)), dma((HEADS,)), dma((HEADS,)), dma((HEADS,)),
            dma((HEADS,)), dma((HEADS,)), dma((HEADS,)), dma((HEADS,)), dma((HEADS,)),
            dma((HEADS,)), dma((HEADS,)), dma((HEADS,)), dma((HEADS,)), dma((HEADS,)),
            dma((HEADS,)), dma((HEADS,)), dma((HEADS,)), dma((HEADS,)),
            dma((4,)), dma((4,)), dma((GZ,)), dma((GZ,)), dma((POS - 1,)), dma((POS - 1,)),
            pltpu.SemaphoreType.REGULAR((3,)), pltpu.SemaphoreType.REGULAR((4,)),
            pltpu.VMEM((8, DIM), F32), pltpu.SMEM((1, 8), jnp.int32), dma((2,)),
        ],
        compiler_params=pltpu.CompilerParams(
            collective_id=1, has_side_effects=True, vmem_limit_bytes=60 * 1024 * 1024
        ),
        name="layer",
    )(key_rows, value_rows, query_rows, cotangent, norm_gain.reshape(8, DIM), doc_starts)
    rows = jax.ShapeDtypeStruct((1, ROWS, 8192), BF16)
    grad_q, grad_k, grad_v, gain = pl.pallas_call(
        place,
        out_shape=(rows, rows, rows, jax.ShapeDtypeStruct((8, DIM), F32)),
        in_specs=[vmem, vmem],
        out_specs=(anywhere, anywhere, anywhere, vmem),
        scratch_shapes=[dma((3,))],
        name="place",
    )(grads, gain_sum)
    return grad_q, grad_k, grad_v, gain.reshape(8 * DIM)


def solution(mesh):
    rows = P("dp", ("seq", "tensor"), None)
    return jax.shard_map(
        local,
        mesh=mesh,
        in_specs=(rows, rows, rows, rows, P("tensor"), P("dp", None)),
        out_specs=(rows, rows, rows, P("tensor")),
        check_vma=False,
    )
```
